32 devices in a mesh: seq: 4 (over x, core), fsdp: 8 (over z, y).
Axes of the slice: x: 2, y: 2, z: 4, core: 2. Of those that a mesh axis runs over, the one named last changes fastest.
Arguments:
- queries: bfloat16 [8, 512, 3072], P('fsdp', 'seq'), may hold values from -6 to 6
- attn_keys: bfloat16 [8, 512, 3072], P('fsdp', 'seq'), may hold values from -6 to 6
- attn_values: bfloat16 [8, 512, 3072], P('fsdp', 'seq'), may hold values from -6 to 6
- grad_out: bfloat16 [8, 512, 6144], P('fsdp', 'seq'), may hold values from -6 to 6
- out_weight: bfloat16 [3072, 6144], P('seq', 'fsdp'), may hold values from -0.109375 to 0.109375
Outputs:
- grad_queries: bfloat16 [8, 512, 3072], P('fsdp', 'seq')
- grad_keys: bfloat16 [8, 512, 3072], P('fsdp', 'seq')
- grad_values: bfloat16 [8, 512, 3072], P('fsdp', 'seq')
- grad_weight: float32 [3072, 6144], P('seq', 'fsdp')
The draws below stay inside these ranges and needn't reach their ends.
All inputs are finite; a program needn't handle non-finite values.
Results may differ from the reference program's by a relative error of at most 0.013.
Values may be sent and summed in bfloat16 or wider, within the bound.
A program may use at most 128 MiB of HBM per device.

```python
import jax
import jax.numpy as jnp
from jax import lax

D = 6144
HEADS = 24
HEAD_DIM = 128
HQ = 3072
LEN = 512
SEQS = 8


def draw_queries(key, part):
    key = jax.random.fold_in(key, 31)
    base = jax.random.truncated_normal(key, -4.0, 4.0, (SEQS, LEN, HQ), jnp.float32)
    return base.astype(jnp.bfloat16)


def draw_attn_keys(key, part):
    key = jax.random.fold_in(key, 47)
    base = jax.random.truncated_normal(key, -4.0, 4.0, (SEQS, LEN, HQ), jnp.float32)
    return base.astype(jnp.bfloat16)


def strengthened(values, stream_key, source, target, parts, factor):
    owner, partner = [(jnp.arange(values.shape[dim]) // (values.shape[dim] // parts)).reshape([-1 if axis == dim else 1 for axis in range(values.ndim)]) for dim in (source, target)]
    chosen = jax.random.permutation(stream_key, parts)[partner]
    strong = (owner == chosen) | (owner == (partner + parts // 2) % parts)
    return jnp.where(strong, factor * values, values)


def shard_levels(rng, shape, split, low, top_value):
    def one(axis_at, blocks):
        draws = jax.random.uniform(jax.random.fold_in(jax.random.fold_in(rng, 6), axis_at), (blocks,), jnp.float32, low / len(split), top_value / len(split))
        return jnp.repeat(jnp.exp(draws), shape[axis_at] // blocks).reshape((-1,) + (1,) * (len(shape) - axis_at - 1))

    loudness = one(*split[0])
    for cut in split[1:]:
        loudness = loudness * one(*cut)
    return loudness


def normal_values(own_key, dims, deviation, reach, split=(), kind=jnp.bfloat16):
    values = deviation * jax.random.normal(own_key, dims, jnp.float32)
    if split:
        values = values * shard_levels(own_key, dims, split, -0.22, 0.18)
    return jnp.clip(values, -reach, reach).astype(kind)


def bell_draw_with(rng, shape, spread, reach, cuts, heavy, dtype=jnp.bfloat16):
    values = spread * jax.random.normal(rng, shape, jnp.float32)
    if cuts:
        values = values * shard_levels(rng, shape, cuts, -0.22, 0.18)
    return jnp.clip(strengthened(values, jax.random.fold_in(rng, 3), *heavy), -reach, reach).astype(dtype)


def setup_inputs(seed: int = 0) -> dict:
    key_list = jax.random.split(jax.random.key(seed), 6)
    queries = draw_queries(jax.random.fold_in(key_list[5], 71), 0)
    attn_keys = draw_attn_keys(jax.random.fold_in(key_list[5], 71), 0)
    attn_values = normal_values(key_list[2], (SEQS, LEN, HQ), 1.0, 6.0, ((0, 8), (1, 4)))
    grad_out = bell_draw_with(key_list[3], (SEQS, LEN, D), 1.0, 6.0, ((0, 8), (1, 4)), (0, 2, 8, 2.0))
    out_weight = normal_values(key_list[4], (HQ, D), HQ ** -0.5, 0.109375, ((0, 4), (1, 8)))
    return {"queries": queries, "attn_keys": attn_keys, "attn_values": attn_values, "grad_out": grad_out, "out_weight": out_weight}


def head_pass(items):
    q, k, v, dout = items
    scale = 1.0 / (HEAD_DIM ** 0.5)
    scores = jnp.dot(q, k.T, preferred_element_type=jnp.float32) * scale
    top = jnp.max(scores, axis=1, keepdims=True)
    expo = jnp.exp(scores - top)
    probs = expo / jnp.sum(expo, axis=1, keepdims=True)
    probs_low = probs.astype(jnp.bfloat16)
    attended = jnp.dot(probs_low, v, preferred_element_type=jnp.float32).astype(jnp.bfloat16)
    grad_v = jnp.dot(probs_low.T, dout, preferred_element_type=jnp.float32).astype(jnp.bfloat16)
    grad_probs = jnp.dot(dout, v.T, preferred_element_type=jnp.float32)
    delta = jnp.sum(dout.astype(jnp.float32) * attended.astype(jnp.float32), axis=1, keepdims=True)
    grad_scores = (probs * (grad_probs - delta)).astype(jnp.bfloat16)
    grad_q = (jnp.dot(grad_scores, k, preferred_element_type=jnp.float32) * scale).astype(jnp.bfloat16)
    grad_k = (jnp.dot(grad_scores.T, q, preferred_element_type=jnp.float32) * scale).astype(jnp.bfloat16)
    return attended, grad_q, grad_k, grad_v


def split_heads(array):
    return array.reshape(SEQS, LEN, HEADS, HEAD_DIM).transpose(0, 2, 1, 3).reshape(SEQS * HEADS, LEN, HEAD_DIM)


def join_heads(array):
    return array.reshape(SEQS, HEADS, LEN, HEAD_DIM).transpose(0, 2, 1, 3).reshape(SEQS, LEN, HQ)


def reference(queries, attn_keys, attn_values, grad_out, out_weight):
    flat_grad = grad_out.reshape(SEQS * LEN, D)
    dout = jnp.dot(flat_grad, out_weight.T, preferred_element_type=jnp.float32).astype(jnp.bfloat16)
    dout = dout.reshape(SEQS, LEN, HQ)
    attended, grad_q, grad_k, grad_v = lax.map(head_pass, (split_heads(queries), split_heads(attn_keys), split_heads(attn_values), split_heads(dout)))
    attended = join_heads(attended)
    grad_weight = jnp.dot(attended.reshape(SEQS * LEN, HQ).T, flat_grad, preferred_element_type=jnp.float32)
    return join_heads(grad_q), join_heads(grad_k), join_heads(grad_v), grad_weight
```

```python
import jax
import jax.numpy as jnp
from jax import lax
from jax.experimental import pallas as pl
from jax.experimental.pallas import tpu as pltpu
from jax.sharding import PartitionSpec as P

HEAD_DIM = 128
TILE = 256
MESH = pl.DeviceIdType.MESH
F32, BF16 = jnp.float32, jnp.bfloat16
NT = (((1,), (1,)), ((), ()))
TN = (((0,), (0,)), ((), ()))


def kernel(
    q_ref, k_ref, v_ref, go_ref, w_ref,
    gq_out, gk_out, gv_out, gw_out,
    qkv, g, w, att, probs, keep, psend, pgot, zsend, zgot, dout, grads, gwsend, gwgot,
    send, recv, local,
):
    s, f = lax.axis_index("seq"), lax.axis_index("fsdp")
    tokens = q_ref.shape[1]
    width = w_ref.shape[0]
    block = w_ref.shape[1]
    heads = width // HEAD_DIM
    scale = 1.0 / HEAD_DIM**0.5
    core = s + 1 - 2 * (s % 2)
    across = s + 2 - 4 * (s // 2)
    both = core + 2 - 4 * (core // 2)
    f_y = f + 1 - 2 * (f % 2)
    f_z = f + 2 - 4 * ((f // 2) % 2)
    f_yz = f_z + 1 - 2 * (f_z % 2)

    def other_half(i):
        return i + 4 - 8 * (i // 4)

    tok_peer = [None] + [{"seq": i, "fsdp": f} for i in (core, across, both)]
    tok_id = [s, core, across, both]
    row_peer = [None] + [{"seq": s, "fsdp": i} for i in (f_y, f_z, f_yz)]
    row_id = [f, f_y, f_z, f_yz]
    far = {"seq": s, "fsdp": other_half(f)}

    barrier = pltpu.get_barrier_semaphore()
    peers = tok_peer[1:] + row_peer[1:] + [far]
    for peer in peers:
        pl.semaphore_signal(barrier, inc=1, device_id=peer, device_id_type=MESH)
    pl.semaphore_wait(barrier, len(peers))

    count = [0, 0]
    pending = []

    def push(src, dst, peer):
        i = count[0]
        count[0] += 1
        copy = pltpu.make_async_remote_copy(
            src_ref=src, dst_ref=dst, send_sem=send.at[i], recv_sem=recv.at[i],
            device_id=peer, device_id_type=MESH,
        )
        copy.start()
        pending.append(copy)
        return copy

    def here(src, dst):
        i = count[1]
        count[1] += 1
        copy = pltpu.make_async_copy(src, dst, local.at[i])
        copy.start()
        return copy

    def cols(i, size):
        return pl.ds(pl.multiple_of(i * size, 128), size)

    def rows(t):
        return pl.ds(t * tokens, tokens)

    own = []
    for c in range(2):
        owner = f if c == 0 else other_half(f)
        own.append(here(go_ref.at[0, :, cols(owner, block)], g.at[0, rows(0), pl.ds(c * block, block)]))
    got_g = {}
    for r in (3, 1, 2):
        for c in range(2):
            owner = row_id[r] if c == 0 else other_half(row_id[r])
            got_g[r, c] = push(
                go_ref.at[0, :, cols(owner, block)], g.at[r, rows(0), pl.ds(c * block, block)], row_peer[r]
            )
    got_w = push(w_ref, w.at[:, pl.ds(block, block)], far)
    own_w = here(w_ref, w.at[:, pl.ds(0, block)])
    got_qkv, own_qkv = [], []
    for a, ref in enumerate((q_ref, k_ref, v_ref)):
        for t in (2, 3, 1):
            got_qkv.append(push(ref.at[0, :, cols(tok_id[t], width)], qkv.at[a, rows(t)], tok_peer[t]))
        own_qkv.append(here(ref.at[0, :, cols(s, width)], qkv.at[a, rows(0)]))

    got_g2 = {}

    def spread(r):
        for t in (2, 1):
            got_g2[r, t] = push(g.at[r, rows(0)], g.at[r, rows(t)], tok_peer[t])

    for copy in own:
        copy.wait()
    spread(0)
    for r in (1, 2, 3):
        got_g[r, 0].wait_recv()
        got_g[r, 1].wait_recv()
        spread(r)

    for copy in own_qkv:
        copy.wait()
    for copy in got_qkv:
        copy.wait_recv()

    def forward(h, carry):
        hc = cols(h, HEAD_DIM)
        scores = lax.dot_general(qkv[0, :, hc], qkv[1, :, hc], NT, preferred_element_type=F32) * scale
        expo = jnp.exp(scores - jnp.max(scores, axis=1, keepdims=True))
        p = expo / jnp.sum(expo, axis=1, keepdims=True)
        probs[h] = p
        att[0, :, hc] = jnp.dot(p.astype(BF16), qkv[2, :, hc], preferred_element_type=F32).astype(BF16)
        return carry

    chunks = width // TILE
    per = TILE // HEAD_DIM
    got_att = {}
    for c in range(chunks):
        lax.fori_loop(c * per, (c + 1) * per, forward, 0)
        cc = pl.ds(c * TILE, TILE)
        got_att[1, c] = push(att.at[0, :, cc], att.at[1, :, cc], row_peer[1])
        got_att[2, c] = push(att.at[0, :, cc], att.at[2, :, cc], row_peer[2])

    for r in range(4):
        got_g2[r, 2].wait_recv()
        got_g2[r, 3] = push(g.at[r, rows(2)], g.at[r, rows(3)], tok_peer[1])
    own_w.wait()
    got_w.wait_recv()

    def partial(r, c):
        return lax.dot_general(g[r], w[pl.ds(c * TILE, TILE), :], NT, preferred_element_type=F32)

    def whole_rows(r):
        got_g2[r, 1].wait_recv()
        got_g2[r, 3].wait_recv()

    got_p = {}
    whole_rows(3)
    whole_rows(1)
    for c in range(chunks):
        cc = pl.ds(c * TILE, TILE)
        for slot, r in ((1, 3), (0, 1)):
            psend[slot, :, cc] = partial(r, c).astype(BF16)
            got_p[slot, c] = push(psend.at[slot, :, cc], pgot.at[slot, :, cc], row_peer[1])
    whole_rows(2)
    whole_rows(0)
    for c in range(chunks):
        cc = pl.ds(c * TILE, TILE)
        keep[1, :, cc] = partial(2, c)
        keep[0, :, cc] = partial(0, c)
        got_att[2, c].wait_recv()
        got_att[3, c] = push(att.at[2, :, cc], att.at[3, :, cc], row_peer[1])

    for c in range(chunks):
        got_att[1, c].wait_recv()
        got_att[3, c].wait_recv()

    def weight_tile(start):
        total = jnp.zeros((width, TILE), F32)
        for r in range(4):
            total += lax.dot_general(att[r], g[r, :, pl.ds(start, TILE)], TN, preferred_element_type=F32)
        return total

    got_gw = []
    for c in range(block // TILE):
        cc = pl.ds(c * TILE, TILE)
        gwsend[:, cc] = weight_tile(block + c * TILE).astype(BF16)
        got_gw.append(push(gwsend.at[:, cc], gwgot.at[:, cc], far))

    got_z = []
    for c in range(chunks):
        cc = pl.ds(c * TILE, TILE)
        got_p[1, c].wait_recv()
        zsend[:, cc] = (keep[1, :, cc] + pgot[1, :, cc].astype(F32)).astype(BF16)
        got_z.append(push(zsend.at[:, cc], zgot.at[:, cc], row_peer[2]))

    for c in range(block // TILE):
        gw_out[:, pl.ds(c * TILE, TILE)] = weight_tile(c * TILE)

    outs = (gq_out, gk_out, gv_out)
    base = count[0]
    count[0] += 9

    def home(a, t, hc, start, size):
        i = base + a * 3 + t - 1
        return pltpu.make_async_remote_copy(
            src_ref=grads.at[a, rows(t), hc],
            dst_ref=outs[a].at[0, :, pl.ds(pl.multiple_of(start, 128), size)],
            send_sem=send.at[i], recv_sem=recv.at[i],
            device_id=tok_peer[t], device_id_type=MESH,
        )

    def backward(h, carry):
        hc = cols(h, HEAD_DIM)
        q, k, v, do = qkv[0, :, hc], qkv[1, :, hc], qkv[2, :, hc], dout[:, hc]
        p = probs[h]
        delta = jnp.sum(do.astype(F32) * att[0, :, hc].astype(F32), axis=1, keepdims=True)
        grad_p = lax.dot_general(do, v, NT, preferred_element_type=F32)
        grad_s = (p * (grad_p - delta)).astype(BF16)
        grads[0, :, hc] = (jnp.dot(grad_s, k, preferred_element_type=F32) * scale).astype(BF16)
        grads[1, :, hc] = (lax.dot_general(grad_s, q, TN, preferred_element_type=F32) * scale).astype(BF16)
        grads[2, :, hc] = lax.dot_general(p.astype(BF16), do, TN, preferred_element_type=F32).astype(BF16)
        for a in range(3):
            for t in (2, 3, 1):
                home(a, t, hc, s * width + h * HEAD_DIM, HEAD_DIM).start()
        return carry

    for c in range(chunks):
        cc = pl.ds(c * TILE, TILE)
        got_p[0, c].wait_recv()
        got_z[c].wait_recv()
        dout[:, cc] = (keep[0, :, cc] + pgot[0, :, cc].astype(F32) + zgot[:, cc].astype(F32)).astype(BF16)
        lax.fori_loop(c * per, (c + 1) * per, backward, 0)

    last = [here(grads.at[a, rows(0)], outs[a].at[0, :, cols(s, width)]) for a in range(3)]
    for copy in got_gw:
        copy.wait_recv()
    gw_out[...] += gwgot[...].astype(F32)
    for a in range(3):
        for t in (1, 2, 3):
            whole = home(a, t, pl.ds(0, width), s * width, width)
            whole.wait_send()
            whole.wait_recv()
    for copy in last:
        copy.wait()
    for copy in pending:
        copy.wait_send()


def fused(queries, attn_keys, attn_values, grad_out, out_weight):
    tokens = queries.shape[1]
    length = tokens * lax.axis_size("seq")
    width, block = out_weight.shape
    heads = width // HEAD_DIM
    any_spec = pl.BlockSpec(memory_space=pl.ANY)
    flops = 4 * length * width * grad_out.shape[2] + 12 * heads * length * length * HEAD_DIM
    return pl.pallas_call(
        kernel,
        out_shape=(
            jax.ShapeDtypeStruct(queries.shape, BF16),
            jax.ShapeDtypeStruct(queries.shape, BF16),
            jax.ShapeDtypeStruct(queries.shape, BF16),
            jax.ShapeDtypeStruct(out_weight.shape, F32),
        ),
        in_specs=[any_spec] * 5,
        out_specs=(any_spec, any_spec, any_spec, pl.BlockSpec(memory_space=pltpu.VMEM)),
        scratch_shapes=[
            pltpu.VMEM((3, length, width), BF16),
            pltpu.VMEM((4, length, 2 * block), BF16),
            pltpu.VMEM((width, 2 * block), BF16),
            pltpu.VMEM((4, length, width), BF16),
            pltpu.VMEM((heads, length, length), F32),
            pltpu.VMEM((2, length, width), F32),
            pltpu.VMEM((2, length, width), BF16),
            pltpu.VMEM((2, length, width), BF16),
            pltpu.VMEM((length, width), BF16),
            pltpu.VMEM((length, width), BF16),
            pltpu.VMEM((length, width), BF16),
            pltpu.VMEM((3, length, width), BF16),
            pltpu.VMEM((width, block), BF16),
            pltpu.VMEM((width, block), BF16),
            pltpu.SemaphoreType.DMA((72,)),
            pltpu.SemaphoreType.DMA((72,)),
            pltpu.SemaphoreType.DMA((16,)),
        ],
        compiler_params=pltpu.CompilerParams(
            collective_id=0, has_side_effects=True, vmem_limit_bytes=60 * 1024 * 1024
        ),
        cost_estimate=pl.CostEstimate(flops=flops, bytes_accessed=20 * 1024 * 1024, transcendentals=0),
    )(queries, attn_keys, attn_values, grad_out, out_weight)


def head_pass(q, k, v, dout):
    scale = 1.0 / q.shape[1] ** 0.5
    scores = jnp.dot(q, k.T, preferred_element_type=F32) * scale
    expo = jnp.exp(scores - jnp.max(scores, axis=1, keepdims=True))
    probs = expo / jnp.sum(expo, axis=1, keepdims=True)
    probs_low = probs.astype(BF16)
    attended = jnp.dot(probs_low, v, preferred_element_type=F32).astype(BF16)
    grad_v = jnp.dot(probs_low.T, dout, preferred_element_type=F32).astype(BF16)
    grad_probs = jnp.dot(dout, v.T, preferred_element_type=F32)
    delta = jnp.sum(dout.astype(F32) * attended.astype(F32), axis=1, keepdims=True)
    grad_scores = (probs * (grad_probs - delta)).astype(BF16)
    grad_q = (jnp.dot(grad_scores, k, preferred_element_type=F32) * scale).astype(BF16)
    grad_k = (jnp.dot(grad_scores.T, q, preferred_element_type=F32) * scale).astype(BF16)
    return attended, grad_q, grad_k, grad_v


def collectives(queries, attn_keys, attn_values, grad_out, out_weight):
    width = queries.shape[2] // lax.axis_size("seq")
    q, k, v = (
        lax.all_to_all(x, "seq", split_axis=2, concat_axis=1, tiled=True)[0]
        for x in (queries, attn_keys, attn_values)
    )
    every_rows = lax.all_gather(grad_out, "seq", axis=1, tiled=True)
    flat_rows = every_rows.reshape(-1, every_rows.shape[2])
    weight = lax.all_gather(out_weight, "fsdp", axis=1, tiled=True)
    dout = lax.dot_general(flat_rows, weight, NT, preferred_element_type=F32).astype(BF16)
    pieces = []
    for lower in range(0, width, HEAD_DIM):
        here = slice(lower, lower + HEAD_DIM)
        pieces.append(head_pass(q[:, here], k[:, here], v[:, here], dout[:, here]))
    attended = jnp.concatenate([item[0] for item in pieces], axis=1)
    grads = [
        lax.all_to_all(
            jnp.concatenate([item[i] for item in pieces], axis=1)[None],
            "seq", split_axis=1, concat_axis=2, tiled=True,
        )
        for i in (1, 2, 3)
    ]
    whole = lax.dot_general(attended, flat_rows, TN, preferred_element_type=F32)
    return (*grads, lax.psum_scatter(whole, "fsdp", scatter_dimension=1, tiled=True))


def shards(queries, attn_keys, attn_values, grad_out, out_weight):
    width, block = out_weight.shape
    fits = lax.axis_size("seq") == 4 and lax.axis_size("fsdp") == 8
    if fits and queries.shape[0] == 1 and queries.shape[1] % 16 == 0 and width % TILE == 0 and block % TILE == 0:
        return fused(queries, attn_keys, attn_values, grad_out, out_weight)
    return collectives(queries, attn_keys, attn_values, grad_out, out_weight)


def solution(mesh):
    return jax.shard_map(
        shards,
        mesh=mesh,
        in_specs=(
            P("fsdp", "seq", None),
            P("fsdp", "seq", None),
            P("fsdp", "seq", None),
            P("fsdp", "seq", None),
            P("seq", "fsdp"),
        ),
        out_specs=(
            P("fsdp", "seq", None),
            P("fsdp", "seq", None),
            P("fsdp", "seq", None),
            P("seq", "fsdp"),
        ),
        check_vma=False,
    )
```

```python
import jax
import jax.numpy as jnp
from jax import lax
from jax.experimental import pallas as pl
from jax.experimental.pallas import tpu as pltpu
from jax.sharding import PartitionSpec as P

HEAD_DIM = 128
TILE = 256
MESH = pl.DeviceIdType.MESH
F32, BF16 = jnp.float32, jnp.bfloat16
NT = (((1,), (1,)), ((), ()))
TN = (((0,), (0,)), ((), ()))


def kernel(
    q_ref, k_ref, v_ref, go_ref, w_ref,
    gq_out, gk_out, gv_out, gw_out,
    qkv, g, w, att, probs, keep, psend, pgot, zsend, zgot, dout, grads, gwsend, gwgot,
    send, recv, local,
):
    s, f = lax.axis_index("seq"), lax.axis_index("fsdp")
    tokens = q_ref.shape[1]
    width = w_ref.shape[0]
    block = w_ref.shape[1]
    heads = width // HEAD_DIM
    scale = 1.0 / HEAD_DIM**0.5
    core = s + 1 - 2 * (s % 2)
    across = s + 2 - 4 * (s // 2)
    both = core + 2 - 4 * (core // 2)
    f_y = f + 1 - 2 * (f % 2)
    f_z = f + 2 - 4 * ((f // 2) % 2)
    f_yz = f_z + 1 - 2 * (f_z % 2)

    def other_half(i):
        return i + 4 - 8 * (i // 4)

    tok_peer = [None] + [{"seq": i, "fsdp": f} for i in (core, across, both)]
    tok_id = [s, core, across, both]
    row_peer = [None] + [{"seq": s, "fsdp": i} for i in (f_y, f_z, f_yz)]
    row_id = [f, f_y, f_z, f_yz]
    far = {"seq": s, "fsdp": other_half(f)}

    barrier = pltpu.get_barrier_semaphore()
    peers = tok_peer[1:] + row_peer[1:] + [far]
    for peer in peers:
        pl.semaphore_signal(barrier, inc=1, device_id=peer, device_id_type=MESH)
    pl.semaphore_wait(barrier, len(peers))

    count = [0, 0]
    pending = []

    def push(src, dst, peer):
        i = count[0]
        count[0] += 1
        copy = pltpu.make_async_remote_copy(
            src_ref=src, dst_ref=dst, send_sem=send.at[i], recv_sem=recv.at[i],
            device_id=peer, device_id_type=MESH,
        )
        copy.start()
        pending.append(copy)
        return copy

    def here(src, dst):
        i = count[1]
        count[1] += 1
        copy = pltpu.make_async_copy(src, dst, local.at[i])
        copy.start()
        return copy

    def cols(i, size):
        return pl.ds(pl.multiple_of(i * size, 128), size)

    def rows(t):
        return pl.ds(t * tokens, tokens)

    own = []
    for c in range(2):
        owner = f if c == 0 else other_half(f)
        own.append(here(go_ref.at[0, :, cols(owner, block)], g.at[0, rows(0), pl.ds(c * block, block)]))
    got_g = {}
    for r in (3, 1, 2):
        for c in range(2):
            owner = row_id[r] if c == 0 else other_half(row_id[r])
            got_g[r, c] = push(
                go_ref.at[0, :, cols(owner, block)], g.at[r, rows(0), pl.ds(c * block, block)], row_peer[r]
            )
    chunks = width // TILE
    per = TILE // HEAD_DIM
    got_qkv, own_qkv = {}, []
    for c in range(chunks):
        cc = pl.ds(c * TILE, TILE)
        got_qkv[c] = []
        for a, ref in enumerate((q_ref, k_ref, v_ref)):
            for t in (2, 3, 1):
                start = pl.multiple_of(tok_id[t] * width + c * TILE, 128)
                got_qkv[c].append(
                    push(ref.at[0, :, pl.ds(start, TILE)], qkv.at[a, rows(t), cc], tok_peer[t])
                )
    for a, ref in enumerate((q_ref, k_ref, v_ref)):
        own_qkv.append(here(ref.at[0, :, cols(s, width)], qkv.at[a, rows(0)]))
    got_w = push(w_ref, w.at[:, pl.ds(block, block)], far)
    own_w = here(w_ref, w.at[:, pl.ds(0, block)])

    got_g2 = {}

    def spread(r):
        for t in (2, 1):
            got_g2[r, t] = push(g.at[r, rows(0)], g.at[r, rows(t)], tok_peer[t])

    for copy in own + own_qkv:
        copy.wait()

    def forward(h, carry):
        hc = cols(h, HEAD_DIM)
        scores = lax.dot_general(qkv[0, :, hc], qkv[1, :, hc], NT, preferred_element_type=F32) * scale
        expo = jnp.exp(scores - jnp.max(scores, axis=1, keepdims=True))
        p = expo / jnp.sum(expo, axis=1, keepdims=True)
        probs[h] = p
        att[0, :, hc] = jnp.dot(p.astype(BF16), qkv[2, :, hc], preferred_element_type=F32).astype(BF16)
        return carry

    order = (0, 3, 1, 2)
    groups = [order[4 * c // chunks : 4 * (c + 1) // chunks] for c in range(chunks)]
    got_att = {}
    for c in range(chunks):
        for copy in got_qkv[c]:
            copy.wait_recv()
        for r in groups[c]:
            if r:
                got_g[r, 0].wait_recv()
                got_g[r, 1].wait_recv()
            spread(r)
        lax.fori_loop(c * per, (c + 1) * per, forward, 0)
        cc = pl.ds(c * TILE, TILE)
        got_att[1, c] = push(att.at[0, :, cc], att.at[1, :, cc], row_peer[1])
        got_att[2, c] = push(att.at[0, :, cc], att.at[2, :, cc], row_peer[2])

    def across_done(r):
        got_g2[r, 2].wait_recv()
        got_g2[r, 3] = push(g.at[r, rows(2)], g.at[r, rows(3)], tok_peer[1])

    def relay(c):
        got_att[2, c].wait_recv()
        cc = pl.ds(c * TILE, TILE)
        got_att[3, c] = push(att.at[2, :, cc], att.at[3, :, cc], row_peer[1])

    for c in range(chunks - 1):
        relay(c)
    for r in order[:3]:
        across_done(r)
    own_w.wait()
    got_w.wait_recv()

    def partial(r, c):
        return lax.dot_general(g[r], w[pl.ds(c * TILE, TILE), :], NT, preferred_element_type=F32)

    def whole_rows(r):
        got_g2[r, 1].wait_recv()
        got_g2[r, 3].wait_recv()

    got_p = {}
    for slot, r in ((1, 3), (0, 1)):
        whole_rows(r)
        for c in range(chunks):
            cc = pl.ds(c * TILE, TILE)
            psend[slot, :, cc] = partial(r, c).astype(BF16)
            got_p[slot, c] = push(psend.at[slot, :, cc], pgot.at[slot, :, cc], row_peer[1])
        if r == 3:
            relay(chunks - 1)
            across_done(2)
    for slot, r in ((1, 2), (0, 0)):
        whole_rows(r)
        for c in range(chunks):
            keep[slot, :, pl.ds(c * TILE, TILE)] = partial(r, c)

    for c in range(chunks):
        got_att[1, c].wait_recv()
        got_att[3, c].wait_recv()

    def weight_tile(start):
        total = jnp.zeros((width, TILE), F32)
        for r in range(4):
            total += lax.dot_general(att[r], g[r, :, pl.ds(start, TILE)], TN, preferred_element_type=F32)
        return total

    got_gw = []
    for c in range(block // TILE):
        cc = pl.ds(c * TILE, TILE)
        gwsend[:, cc] = weight_tile(block + c * TILE).astype(BF16)
        got_gw.append(push(gwsend.at[:, cc], gwgot.at[:, cc], far))

    got_z = []
    for c in range(chunks):
        cc = pl.ds(c * TILE, TILE)
        got_p[1, c].wait_recv()
        zsend[:, cc] = (keep[1, :, cc] + pgot[1, :, cc].astype(F32)).astype(BF16)
        got_z.append(push(zsend.at[:, cc], zgot.at[:, cc], row_peer[2]))

    for c in range(block // TILE):
        gw_out[:, pl.ds(c * TILE, TILE)] = weight_tile(c * TILE)

    outs = (gq_out, gk_out, gv_out)
    base = count[0]
    count[0] += 9

    def home(a, t, hc, start, size):
        i = base + a * 3 + t - 1
        return pltpu.make_async_remote_copy(
            src_ref=grads.at[a, rows(t), hc],
            dst_ref=outs[a].at[0, :, pl.ds(pl.multiple_of(start, 128), size)],
            send_sem=send.at[i], recv_sem=recv.at[i],
            device_id=tok_peer[t], device_id_type=MESH,
        )

    def backward(h, carry):
        hc = cols(h, HEAD_DIM)
        q, k, v, do = qkv[0, :, hc], qkv[1, :, hc], qkv[2, :, hc], dout[:, hc]
        p = probs[h]
        delta = jnp.sum(do.astype(F32) * att[0, :, hc].astype(F32), axis=1, keepdims=True)
        grad_p = lax.dot_general(do, v, NT, preferred_element_type=F32)
        grad_s = (p * (grad_p - delta)).astype(BF16)
        grads[0, :, hc] = (jnp.dot(grad_s, k, preferred_element_type=F32) * scale).astype(BF16)
        grads[1, :, hc] = (lax.dot_general(grad_s, q, TN, preferred_element_type=F32) * scale).astype(BF16)
        grads[2, :, hc] = lax.dot_general(p.astype(BF16), do, TN, preferred_element_type=F32).astype(BF16)
        for a in range(3):
            for t in (2, 3, 1):
                home(a, t, hc, s * width + h * HEAD_DIM, HEAD_DIM).start()
        return carry

    for c in range(chunks):
        cc = pl.ds(c * TILE, TILE)
        got_p[0, c].wait_recv()
        got_z[c].wait_recv()
        dout[:, cc] = (keep[0, :, cc] + pgot[0, :, cc].astype(F32) + zgot[:, cc].astype(F32)).astype(BF16)
        lax.fori_loop(c * per, (c + 1) * per, backward, 0)

    last = [here(grads.at[a, rows(0)], outs[a].at[0, :, cols(s, width)]) for a in range(3)]
    for copy in got_gw:
        copy.wait_recv()
    gw_out[...] += gwgot[...].astype(F32)
    for a in range(3):
        for t in (1, 2, 3):
            whole = home(a, t, pl.ds(0, width), s * width, width)
            whole.wait_send()
            whole.wait_recv()
    for copy in last:
        copy.wait()
    for copy in pending:
        copy.wait_send()


def fused(queries, attn_keys, attn_values, grad_out, out_weight):
    tokens = queries.shape[1]
    length = tokens * lax.axis_size("seq")
    width, block = out_weight.shape
    heads = width // HEAD_DIM
    any_spec = pl.BlockSpec(memory_space=pl.ANY)
    flops = 4 * length * width * grad_out.shape[2] + 12 * heads * length * length * HEAD_DIM
    return pl.pallas_call(
        kernel,
        out_shape=(
            jax.ShapeDtypeStruct(queries.shape, BF16),
            jax.ShapeDtypeStruct(queries.shape, BF16),
            jax.ShapeDtypeStruct(queries.shape, BF16),
            jax.ShapeDtypeStruct(out_weight.shape, F32),
        ),
        in_specs=[any_spec] * 5,
        out_specs=(any_spec, any_spec, any_spec, pl.BlockSpec(memory_space=pltpu.VMEM)),
        scratch_shapes=[
            pltpu.VMEM((3, length, width), BF16),
            pltpu.VMEM((4, length, 2 * block), BF16),
            pltpu.VMEM((width, 2 * block), BF16),
            pltpu.VMEM((4, length, width), BF16),
            pltpu.VMEM((heads, length, length), F32),
            pltpu.VMEM((2, length, width), F32),
            pltpu.VMEM((2, length, width), BF16),
            pltpu.VMEM((2, length, width), BF16),
            pltpu.VMEM((length, width), BF16),
            pltpu.VMEM((length, width), BF16),
            pltpu.VMEM((length, width), BF16),
            pltpu.VMEM((3, length, width), BF16),
            pltpu.VMEM((width, block), BF16),
            pltpu.VMEM((width, block), BF16),
            pltpu.SemaphoreType.DMA((96,)),
            pltpu.SemaphoreType.DMA((96,)),
            pltpu.SemaphoreType.DMA((16,)),
        ],
        compiler_params=pltpu.CompilerParams(
            collective_id=0, has_side_effects=True, vmem_limit_bytes=60 * 1024 * 1024
        ),
        cost_estimate=pl.CostEstimate(flops=flops, bytes_accessed=20 * 1024 * 1024, transcendentals=0),
    )(queries, attn_keys, attn_values, grad_out, out_weight)


def head_pass(q, k, v, dout):
    scale = 1.0 / q.shape[1] ** 0.5
    scores = jnp.dot(q, k.T, preferred_element_type=F32) * scale
    expo = jnp.exp(scores - jnp.max(scores, axis=1, keepdims=True))
    probs = expo / jnp.sum(expo, axis=1, keepdims=True)
    probs_low = probs.astype(BF16)
    attended = jnp.dot(probs_low, v, preferred_element_type=F32).astype(BF16)
    grad_v = jnp.dot(probs_low.T, dout, preferred_element_type=F32).astype(BF16)
    grad_probs = jnp.dot(dout, v.T, preferred_element_type=F32)
    delta = jnp.sum(dout.astype(F32) * attended.astype(F32), axis=1, keepdims=True)
    grad_scores = (probs * (grad_probs - delta)).astype(BF16)
    grad_q = (jnp.dot(grad_scores, k, preferred_element_type=F32) * scale).astype(BF16)
    grad_k = (jnp.dot(grad_scores.T, q, preferred_element_type=F32) * scale).astype(BF16)
    return attended, grad_q, grad_k, grad_v


def collectives(queries, attn_keys, attn_values, grad_out, out_weight):
    width = queries.shape[2] // lax.axis_size("seq")
    q, k, v = (
        lax.all_to_all(x, "seq", split_axis=2, concat_axis=1, tiled=True)[0]
        for x in (queries, attn_keys, attn_values)
    )
    every_rows = lax.all_gather(grad_out, "seq", axis=1, tiled=True)
    flat_rows = every_rows.reshape(-1, every_rows.shape[2])
    weight = lax.all_gather(out_weight, "fsdp", axis=1, tiled=True)
    dout = lax.dot_general(flat_rows, weight, NT, preferred_element_type=F32).astype(BF16)
    pieces = []
    for lower in range(0, width, HEAD_DIM):
        here = slice(lower, lower + HEAD_DIM)
        pieces.append(head_pass(q[:, here], k[:, here], v[:, here], dout[:, here]))
    attended = jnp.concatenate([item[0] for item in pieces], axis=1)
    grads = [
        lax.all_to_all(
            jnp.concatenate([item[i] for item in pieces], axis=1)[None],
            "seq", split_axis=1, concat_axis=2, tiled=True,
        )
        for i in (1, 2, 3)
    ]
    whole = lax.dot_general(attended, flat_rows, TN, preferred_element_type=F32)
    return (*grads, lax.psum_scatter(whole, "fsdp", scatter_dimension=1, tiled=True))


def shards(queries, attn_keys, attn_values, grad_out, out_weight):
    width, block = out_weight.shape
    fits = lax.axis_size("seq") == 4 and lax.axis_size("fsdp") == 8
    if fits and queries.shape[0] == 1 and queries.shape[1] % 16 == 0 and width % TILE == 0 and block % TILE == 0:
        return fused(queries, attn_keys, attn_values, grad_out, out_weight)
    return collectives(queries, attn_keys, attn_values, grad_out, out_weight)


def solution(mesh):
    return jax.shard_map(
        shards,
        mesh=mesh,
        in_specs=(
            P("fsdp", "seq", None),
            P("fsdp", "seq", None),
            P("fsdp", "seq", None),
            P("fsdp", "seq", None),
            P("seq", "fsdp"),
        ),
        out_specs=(
            P("fsdp", "seq", None),
            P("fsdp", "seq", None),
            P("fsdp", "seq", None),
            P("seq", "fsdp"),
        ),
        check_vma=False,
    )
```

```python
import jax
import jax.numpy as jnp
from jax import lax
from jax.experimental import pallas as pl
from jax.experimental.pallas import tpu as pltpu
from jax.sharding import PartitionSpec as P

HEAD_DIM = 128
LOG2_E = 1.4426950408889634
TILE = 256
MESH = pl.DeviceIdType.MESH
F32, BF16 = jnp.float32, jnp.bfloat16
NT = (((1,), (1,)), ((), ()))
TN = (((0,), (0,)), ((), ()))


def kernel(
    q_ref, k_ref, v_ref, go_ref, w_ref,
    gq_out, gk_out, gv_out, gw_out,
    qkv, g, w, att, probs, keep, psend, pgot, zsend, zgot, dout, grads, gwsend, gwgot,
    send, recv, local,
):
    s, f = lax.axis_index("seq"), lax.axis_index("fsdp")
    tokens = q_ref.shape[1]
    width = w_ref.shape[0]
    block = w_ref.shape[1]
    heads = width // HEAD_DIM
    scale = 1.0 / HEAD_DIM**0.5
    core = s + 1 - 2 * (s % 2)
    across = s + 2 - 4 * (s // 2)
    both = core + 2 - 4 * (core // 2)
    f_y = f + 1 - 2 * (f % 2)
    f_z = f + 2 - 4 * ((f // 2) % 2)
    f_yz = f_z + 1 - 2 * (f_z % 2)

    def other_half(i):
        return i + 4 - 8 * (i // 4)

    tok_peer = [None] + [{"seq": i, "fsdp": f} for i in (core, across, both)]
    tok_id = [s, core, across, both]
    row_peer = [None] + [{"seq": s, "fsdp": i} for i in (f_y, f_z, f_yz)]
    row_id = [f, f_y, f_z, f_yz]
    far = {"seq": s, "fsdp": other_half(f)}

    barrier = pltpu.get_barrier_semaphore()
    peers = tok_peer[1:] + row_peer[1:] + [far]
    for peer in peers:
        pl.semaphore_signal(barrier, inc=1, device_id=peer, device_id_type=MESH)
    pl.semaphore_wait(barrier, len(peers))

    count = [0, 0]
    pending = []

    def push(src, dst, peer):
        i = count[0]
        count[0] += 1
        copy = pltpu.make_async_remote_copy(
            src_ref=src, dst_ref=dst, send_sem=send.at[i], recv_sem=recv.at[i],
            device_id=peer, device_id_type=MESH,
        )
        copy.start()
        pending.append(copy)
        return copy

    def here(src, dst):
        i = count[1]
        count[1] += 1
        copy = pltpu.make_async_copy(src, dst, local.at[i])
        copy.start()
        return copy

    def cols(i, size):
        return pl.ds(pl.multiple_of(i * size, 128), size)

    def rows(t):
        return pl.ds(t * tokens, tokens)

    own = []
    for c in range(2):
        owner = f if c == 0 else other_half(f)
        own.append(here(go_ref.at[0, :, cols(owner, block)], g.at[0, rows(0), pl.ds(c * block, block)]))
    got_g = {}
    for r in (3, 1, 2):
        for c in range(2):
            owner = row_id[r] if c == 0 else other_half(row_id[r])
            got_g[r, c] = push(
                go_ref.at[0, :, cols(owner, block)], g.at[r, rows(0), pl.ds(c * block, block)], row_peer[r]
            )
    chunks = width // TILE
    per = TILE // HEAD_DIM
    got_qkv, own_qkv = {}, []
    for c in range(chunks):
        cc = pl.ds(c * TILE, TILE)
        got_qkv[c] = []
        for a, ref in enumerate((q_ref, k_ref, v_ref)):
            for t in (2, 3, 1):
                start = pl.multiple_of(tok_id[t] * width + c * TILE, 128)
                got_qkv[c].append(
                    push(ref.at[0, :, pl.ds(start, TILE)], qkv.at[a, rows(t), cc], tok_peer[t])
                )
    for a, ref in enumerate((q_ref, k_ref, v_ref)):
        own_qkv.append(here(ref.at[0, :, cols(s, width)], qkv.at[a, rows(0)]))
    got_w = push(w_ref, w.at[:, pl.ds(block, block)], far)
    own_w = here(w_ref, w.at[:, pl.ds(0, block)])

    got_g2 = {}

    def spread(r):
        for t in (2, 1):
            got_g2[r, t] = push(g.at[r, rows(0)], g.at[r, rows(t)], tok_peer[t])

    for copy in own + own_qkv:
        copy.wait()

    def forward(h, carry):
        hc = cols(h, HEAD_DIM)
        scores = lax.dot_general(qkv[1, :, hc], qkv[0, :, hc], NT, preferred_element_type=F32)
        top = jnp.max(scores, axis=0, keepdims=True) * (scale * LOG2_E)
        expo = jnp.exp2(scores * (scale * LOG2_E) - top)
        p = expo * (1.0 / jnp.sum(expo, axis=0, keepdims=True))
        probs[h] = p
        att[0, hc, :] = lax.dot_general(
            qkv[2, :, hc], p.astype(BF16), TN, preferred_element_type=F32
        ).astype(BF16)
        return carry

    order = (0, 3, 1, 2)
    groups = [order[4 * c // chunks : 4 * (c + 1) // chunks] for c in range(chunks)]
    got_att = {}
    for c in range(chunks):
        for copy in got_qkv[c]:
            copy.wait_recv()
        for r in groups[c]:
            if r:
                got_g[r, 0].wait_recv()
                got_g[r, 1].wait_recv()
            spread(r)
        lax.fori_loop(c * per, (c + 1) * per, forward, 0)
        cc = pl.ds(c * TILE, TILE)
        got_att[1, c] = push(att.at[0, cc], att.at[1, cc], row_peer[1])
        got_att[2, c] = push(att.at[0, cc], att.at[2, cc], row_peer[2])

    def across_done(r):
        got_g2[r, 2].wait_recv()
        got_g2[r, 3] = push(g.at[r, rows(2)], g.at[r, rows(3)], tok_peer[1])

    def relay(c):
        got_att[2, c].wait_recv()
        cc = pl.ds(c * TILE, TILE)
        got_att[3, c] = push(att.at[2, cc], att.at[3, cc], row_peer[1])

    for c in range(chunks - 1):
        relay(c)
    for r in order[:3]:
        across_done(r)
    own_w.wait()
    got_w.wait_recv()

    def partial(r, c):
        return lax.dot_general(g[r], w[pl.ds(c * TILE, TILE), :], NT, preferred_element_type=F32)

    def whole_rows(r):
        got_g2[r, 1].wait_recv()
        got_g2[r, 3].wait_recv()

    got_p = {}
    for slot, r in ((1, 3), (0, 1)):
        whole_rows(r)
        for c in range(chunks):
            cc = pl.ds(c * TILE, TILE)
            psend[slot, :, cc] = partial(r, c).astype(BF16)
            got_p[slot, c] = push(psend.at[slot, :, cc], pgot.at[slot, :, cc], row_peer[1])
        if r == 3:
            relay(chunks - 1)
            across_done(2)
    for slot, r in ((1, 2), (0, 0)):
        whole_rows(r)
        for c in range(chunks):
            keep[slot, :, pl.ds(c * TILE, TILE)] = partial(r, c)

    for c in range(chunks):
        got_att[1, c].wait_recv()
        got_att[3, c].wait_recv()

    def weight_tile(start):
        total = jnp.zeros((width, TILE), F32)
        for r in range(4):
            total += jnp.dot(att[r], g[r, :, pl.ds(start, TILE)], preferred_element_type=F32)
        return total

    got_gw = []
    for c in range(block // TILE):
        cc = pl.ds(c * TILE, TILE)
        gwsend[:, cc] = weight_tile(block + c * TILE).astype(BF16)
        got_gw.append(push(gwsend.at[:, cc], gwgot.at[:, cc], far))

    got_z = []
    for c in range(chunks):
        cc = pl.ds(c * TILE, TILE)
        got_p[1, c].wait_recv()
        zsend[:, cc] = (keep[1, :, cc] + pgot[1, :, cc].astype(F32)).astype(BF16)
        got_z.append(push(zsend.at[:, cc], zgot.at[:, cc], row_peer[2]))

    for c in range(block // TILE):
        gw_out[:, pl.ds(c * TILE, TILE)] = weight_tile(c * TILE)

    outs = (gq_out, gk_out, gv_out)
    base = count[0]
    count[0] += 9

    def home(a, t, hc, start, size):
        i = base + a * 3 + t - 1
        return pltpu.make_async_remote_copy(
            src_ref=grads.at[a, rows(t), hc],
            dst_ref=outs[a].at[0, :, pl.ds(pl.multiple_of(start, 128), size)],
            send_sem=send.at[i], recv_sem=recv.at[i],
            device_id=tok_peer[t], device_id_type=MESH,
        )

    def backward(h, carry):
        hc = cols(h, HEAD_DIM)
        q, k, v, do = qkv[0, :, hc], qkv[1, :, hc], qkv[2, :, hc], dout[:, hc]
        p = probs[h]
        delta = jnp.sum(do.astype(F32).T * att[0, hc, :].astype(F32), axis=0, keepdims=True)
        grad_p = lax.dot_general(v, do, NT, preferred_element_type=F32)
        grad_s = (p * (grad_p - delta)).astype(BF16)
        grad_q = lax.dot_general(k, grad_s, TN, preferred_element_type=F32) * scale
        grads[0, :, hc] = grad_q.T.astype(BF16)
        grads[1, :, hc] = (jnp.dot(grad_s, q, preferred_element_type=F32) * scale).astype(BF16)
        grads[2, :, hc] = jnp.dot(p.astype(BF16), do, preferred_element_type=F32).astype(BF16)
        for a in range(3):
            for t in (2, 3, 1):
                home(a, t, hc, s * width + h * HEAD_DIM, HEAD_DIM).start()
        return carry

    for c in range(chunks):
        cc = pl.ds(c * TILE, TILE)
        got_p[0, c].wait_recv()
        got_z[c].wait_recv()
        dout[:, cc] = (keep[0, :, cc] + pgot[0, :, cc].astype(F32) + zgot[:, cc].astype(F32)).astype(BF16)
        lax.fori_loop(c * per, (c + 1) * per, backward, 0)

    last = [here(grads.at[a, rows(0)], outs[a].at[0, :, cols(s, width)]) for a in range(3)]
    for copy in got_gw:
        copy.wait_recv()
    gw_out[...] += gwgot[...].astype(F32)
    for a in range(3):
        for t in (1, 2, 3):
            whole = home(a, t, pl.ds(0, width), s * width, width)
            whole.wait_send()
            whole.wait_recv()
    for copy in last:
        copy.wait()
    for copy in pending:
        copy.wait_send()


def fused(queries, attn_keys, attn_values, grad_out, out_weight):
    tokens = queries.shape[1]
    length = tokens * lax.axis_size("seq")
    width, block = out_weight.shape
    heads = width // HEAD_DIM
    any_spec = pl.BlockSpec(memory_space=pl.ANY)
    flops = 4 * length * width * grad_out.shape[2] + 12 * heads * length * length * HEAD_DIM
    results = pl.pallas_call(
        kernel,
        out_shape=(
            jax.ShapeDtypeStruct(queries.shape, BF16),
            jax.ShapeDtypeStruct(queries.shape, BF16),
            jax.ShapeDtypeStruct(queries.shape, BF16),
            jax.ShapeDtypeStruct(out_weight.shape, F32),
        ),
        in_specs=[any_spec] * 5,
        out_specs=(any_spec, any_spec, any_spec, pl.BlockSpec(memory_space=pltpu.VMEM)),
        scratch_shapes=[
            pltpu.VMEM((3, length, width), BF16),
            pltpu.VMEM((4, length, 2 * block), BF16),
            pltpu.VMEM((width, 2 * block), BF16),
            pltpu.VMEM((4, width, length), BF16),
            pltpu.VMEM((heads, length, length), F32),
            pltpu.VMEM((2, length, width), F32),
            pltpu.VMEM((2, length, width), BF16),
            pltpu.VMEM((2, length, width), BF16),
            pltpu.VMEM((length, width), BF16),
            pltpu.VMEM((length, width), BF16),
            pltpu.VMEM((length, width), BF16),
            pltpu.VMEM((3, length, width), BF16),
            pltpu.VMEM((width, block), BF16),
            pltpu.VMEM((width, block), BF16),
            pltpu.SemaphoreType.DMA((96,)),
            pltpu.SemaphoreType.DMA((96,)),
            pltpu.SemaphoreType.DMA((16,)),
        ],
        compiler_params=pltpu.CompilerParams(
            collective_id=0, has_side_effects=True, vmem_limit_bytes=60 * 1024 * 1024
        ),
        cost_estimate=pl.CostEstimate(flops=flops, bytes_accessed=20 * 1024 * 1024, transcendentals=0),
    )(queries, attn_keys, attn_values, grad_out, out_weight)
    return place(*results)


def place_kernel(*refs):
    for src, dst in zip(refs[:4], refs[4:]):
        dst[...] = src[...]


def place(*results):
    steps = 4
    specs = [pl.BlockSpec((1, x.shape[1] // steps, x.shape[2]), lambda i: (0, i, 0)) for x in results[:3]]
    specs.append(pl.BlockSpec((results[3].shape[0] // steps, results[3].shape[1]), lambda i: (i, 0)))
    return pl.pallas_call(
        place_kernel,
        grid=(steps,),
        out_shape=tuple(jax.ShapeDtypeStruct(x.shape, x.dtype) for x in results),
        in_specs=specs,
        out_specs=tuple(specs),
        compiler_params=pltpu.CompilerParams(vmem_limit_bytes=60 * 1024 * 1024),
    )(*results)


def head_pass(q, k, v, dout):
    scale = 1.0 / q.shape[1] ** 0.5
    scores = jnp.dot(q, k.T, preferred_element_type=F32) * scale
    expo = jnp.exp(scores - jnp.max(scores, axis=1, keepdims=True))
    probs = expo / jnp.sum(expo, axis=1, keepdims=True)
    probs_low = probs.astype(BF16)
    attended = jnp.dot(probs_low, v, preferred_element_type=F32).astype(BF16)
    grad_v = jnp.dot(probs_low.T, dout, preferred_element_type=F32).astype(BF16)
    grad_probs = jnp.dot(dout, v.T, preferred_element_type=F32)
    delta = jnp.sum(dout.astype(F32) * attended.astype(F32), axis=1, keepdims=True)
    grad_scores = (probs * (grad_probs - delta)).astype(BF16)
    grad_q = (jnp.dot(grad_scores, k, preferred_element_type=F32) * scale).astype(BF16)
    grad_k = (jnp.dot(grad_scores.T, q, preferred_element_type=F32) * scale).astype(BF16)
    return attended, grad_q, grad_k, grad_v


def collectives(queries, attn_keys, attn_values, grad_out, out_weight):
    width = queries.shape[2] // lax.axis_size("seq")
    q, k, v = (
        lax.all_to_all(x, "seq", split_axis=2, concat_axis=1, tiled=True)[0]
        for x in (queries, attn_keys, attn_values)
    )
    every_rows = lax.all_gather(grad_out, "seq", axis=1, tiled=True)
    flat_rows = every_rows.reshape(-1, every_rows.shape[2])
    weight = lax.all_gather(out_weight, "fsdp", axis=1, tiled=True)
    dout = lax.dot_general(flat_rows, weight, NT, preferred_element_type=F32).astype(BF16)
    pieces = []
    for lower in range(0, width, HEAD_DIM):
        here = slice(lower, lower + HEAD_DIM)
        pieces.append(head_pass(q[:, here], k[:, here], v[:, here], dout[:, here]))
    attended = jnp.concatenate([item[0] for item in pieces], axis=1)
    grads = [
        lax.all_to_all(
            jnp.concatenate([item[i] for item in pieces], axis=1)[None],
            "seq", split_axis=1, concat_axis=2, tiled=True,
        )
        for i in (1, 2, 3)
    ]
    whole = lax.dot_general(attended, flat_rows, TN, preferred_element_type=F32)
    return (*grads, lax.psum_scatter(whole, "fsdp", scatter_dimension=1, tiled=True))


def shards(queries, attn_keys, attn_values, grad_out, out_weight):
    width, block = out_weight.shape
    fits = lax.axis_size("seq") == 4 and lax.axis_size("fsdp") == 8
    if fits and queries.shape[0] == 1 and queries.shape[1] % 64 == 0 and width % TILE == 0 and block % TILE == 0:
        return fused(queries, attn_keys, attn_values, grad_out, out_weight)
    return collectives(queries, attn_keys, attn_values, grad_out, out_weight)


def solution(mesh):
    return jax.shard_map(
        shards,
        mesh=mesh,
        in_specs=(
            P("fsdp", "seq", None),
            P("fsdp", "seq", None),
            P("fsdp", "seq", None),
            P("fsdp", "seq", None),
            P("seq", "fsdp"),
        ),
        out_specs=(
            P("fsdp", "seq", None),
            P("fsdp", "seq", None),
            P("fsdp", "seq", None),
            P("seq", "fsdp"),
        ),
        check_vma=False,
    )
```

```python
import jax
import jax.numpy as jnp
from jax import lax
from jax.experimental import pallas as pl
from jax.experimental.pallas import tpu as pltpu
from jax.sharding import PartitionSpec as P

HEAD_DIM = 128
LOG2_E = 1.4426950408889634
TILE = 256
MESH = pl.DeviceIdType.MESH
F32, BF16 = jnp.float32, jnp.bfloat16
NT = (((1,), (1,)), ((), ()))
TN = (((0,), (0,)), ((), ()))


def kernel(
    q_ref, k_ref, v_ref, go_ref, w_ref,
    gq_out, gk_out, gv_out, gw_out,
    qkv, g, w, att, probs, keep, psend, pgot, zsend, zgot, dout, grads, gwsend, gwgot,
    send, recv, local,
):
    s, f = lax.axis_index("seq"), lax.axis_index("fsdp")
    tokens = q_ref.shape[1]
    width = w_ref.shape[0]
    block = w_ref.shape[1]
    heads = width // HEAD_DIM
    scale = 1.0 / HEAD_DIM**0.5
    core = s + 1 - 2 * (s % 2)
    across = s + 2 - 4 * (s // 2)
    both = core + 2 - 4 * (core // 2)
    f_y = f + 1 - 2 * (f % 2)
    f_z = f + 4 - 8 * (f // 4)
    f_yz = f_z + 1 - 2 * (f_z % 2)

    def other_half(i):
        return i + 2 - 4 * ((i // 2) % 2)

    tok_peer = [None] + [{"seq": i, "fsdp": f} for i in (core, across, both)]
    tok_id = [s, core, across, both]
    row_peer = [None] + [{"seq": s, "fsdp": i} for i in (f_y, f_z, f_yz)]
    row_id = [f, f_y, f_z, f_yz]
    far = {"seq": s, "fsdp": other_half(f)}

    barrier = pltpu.get_barrier_semaphore()
    peers = tok_peer[1:] + row_peer[1:] + [far]
    for peer in peers:
        pl.semaphore_signal(barrier, inc=1, device_id=peer, device_id_type=MESH)
    pl.semaphore_wait(barrier, len(peers))

    count = [0, 0]
    pending = []

    def push(src, dst, peer):
        i = count[0]
        count[0] += 1
        copy = pltpu.make_async_remote_copy(
            src_ref=src, dst_ref=dst, send_sem=send.at[i], recv_sem=recv.at[i],
            device_id=peer, device_id_type=MESH,
        )
        copy.start()
        pending.append(copy)
        return copy

    def here(src, dst):
        i = count[1]
        count[1] += 1
        copy = pltpu.make_async_copy(src, dst, local.at[i])
        copy.start()
        return copy

    def cols(i, size):
        return pl.ds(pl.multiple_of(i * size, 128), size)

    def rows(t):
        return pl.ds(t * tokens, tokens)

    own = []
    for c in range(2):
        owner = f if c == 0 else other_half(f)
        own.append(here(go_ref.at[0, :, cols(owner, block)], g.at[0, rows(0), pl.ds(c * block, block)]))
    got_g = {}
    for r in (3, 1, 2):
        for c in range(2):
            owner = row_id[r] if c == 0 else other_half(row_id[r])
            got_g[r, c] = push(
                go_ref.at[0, :, cols(owner, block)], g.at[r, rows(0), pl.ds(c * block, block)], row_peer[r]
            )
    chunks = width // TILE
    per = TILE // HEAD_DIM
    got_qkv, own_qkv = {}, []

    def send_qkv(c):
        cc = pl.ds(c * TILE, TILE)
        got_qkv[c] = []
        for a, ref in enumerate((q_ref, k_ref, v_ref)):
            for t in (2, 3, 1):
                start = pl.multiple_of(tok_id[t] * width + c * TILE, 128)
                got_qkv[c].append(
                    push(ref.at[0, :, pl.ds(start, TILE)], qkv.at[a, rows(t), cc], tok_peer[t])
                )

    send_qkv(0)
    for a, ref in enumerate((q_ref, k_ref, v_ref)):
        own_qkv.append(here(ref.at[0, :, cols(s, width)], qkv.at[a, rows(0)]))
    got_w = push(w_ref, w.at[:, pl.ds(block, block)], far)
    own_w = here(w_ref, w.at[:, pl.ds(0, block)])

    got_g2 = {}

    def spread(r):
        for t in (2, 1):
            got_g2[r, t] = push(g.at[r, rows(0)], g.at[r, rows(t)], tok_peer[t])

    for copy in own + own_qkv:
        copy.wait()
    order = (0, 3, 1, 2)
    for r in order:
        if r:
            got_g[r, 0].wait_recv()
            got_g[r, 1].wait_recv()
        spread(r)
    for c in range(1, chunks):
        send_qkv(c)

    def forward(h, carry):
        hc = cols(h, HEAD_DIM)
        scores = lax.dot_general(qkv[1, :, hc], qkv[0, :, hc], NT, preferred_element_type=F32)
        top = jnp.max(scores, axis=0, keepdims=True) * (scale * LOG2_E)
        expo = jnp.exp2(scores * (scale * LOG2_E) - top)
        p = expo * (1.0 / jnp.sum(expo, axis=0, keepdims=True))
        probs[h] = p
        att[0, hc, :] = lax.dot_general(
            qkv[2, :, hc], p.astype(BF16), TN, preferred_element_type=F32
        ).astype(BF16)
        return carry

    got_att = {}

    def attend(c):
        for copy in got_qkv[c]:
            copy.wait_recv()
        lax.fori_loop(c * per, (c + 1) * per, forward, 0)
        cc = pl.ds(c * TILE, TILE)
        got_att[1, c] = push(att.at[0, cc], att.at[1, cc], row_peer[1])
        got_att[2, c] = push(att.at[0, cc], att.at[2, cc], row_peer[2])

    attend(0)

    def across_done(r):
        got_g2[r, 2].wait_recv()
        got_g2[r, 3] = push(g.at[r, rows(2)], g.at[r, rows(3)], tok_peer[1])

    def relay(c):
        got_att[2, c].wait_recv()
        cc = pl.ds(c * TILE, TILE)
        got_att[3, c] = push(att.at[2, cc], att.at[3, cc], row_peer[1])

    for r in order[:3]:
        across_done(r)
    relay(0)
    own_w.wait()
    got_w.wait_recv()

    def partial(r, c):
        return lax.dot_general(g[r], w[pl.ds(c * TILE, TILE), :], NT, preferred_element_type=F32)

    def whole_rows(r):
        got_g2[r, 1].wait_recv()
        got_g2[r, 3].wait_recv()

    got_p = {}
    for slot, r in ((1, 3), (0, 1)):
        whole_rows(r)
        for c in range(chunks):
            cc = pl.ds(c * TILE, TILE)
            psend[slot, :, cc] = partial(r, c).astype(BF16)
            got_p[slot, c] = push(psend.at[slot, :, cc], pgot.at[slot, :, cc], row_peer[1])
        if r == 3:
            across_done(2)
    for slot, r in ((1, 2), (0, 0)):
        whole_rows(r)
        for c in range(chunks):
            keep[slot, :, pl.ds(c * TILE, TILE)] = partial(r, c)

    for c in range(1, chunks):
        attend(c)
    for c in range(1, chunks):
        relay(c)

    got_z = []
    for c in range(chunks):
        cc = pl.ds(c * TILE, TILE)
        got_p[1, c].wait_recv()
        zsend[:, cc] = (keep[1, :, cc] + pgot[1, :, cc].astype(F32)).astype(BF16)
        got_z.append(push(zsend.at[:, cc], zgot.at[:, cc], row_peer[2]))

    outs = (gq_out, gk_out, gv_out)
    base = count[0]
    count[0] += 9

    def home(a, t, hc, start, size):
        i = base + a * 3 + t - 1
        return pltpu.make_async_remote_copy(
            src_ref=grads.at[a, rows(t), hc],
            dst_ref=outs[a].at[0, :, pl.ds(pl.multiple_of(start, 128), size)],
            send_sem=send.at[i], recv_sem=recv.at[i],
            device_id=tok_peer[t], device_id_type=MESH,
        )

    def backward(h, carry):
        hc = cols(h, HEAD_DIM)
        q, k, v, do = qkv[0, :, hc], qkv[1, :, hc], qkv[2, :, hc], dout[:, hc]
        p = probs[h]
        delta = jnp.sum(do.astype(F32).T * att[0, hc, :].astype(F32), axis=0, keepdims=True)
        grad_p = lax.dot_general(v, do, NT, preferred_element_type=F32)
        grad_s = (p * (grad_p - delta)).astype(BF16)
        grad_q = lax.dot_general(k, grad_s, TN, preferred_element_type=F32) * scale
        grads[0, :, hc] = grad_q.T.astype(BF16)
        grads[1, :, hc] = (jnp.dot(grad_s, q, preferred_element_type=F32) * scale).astype(BF16)
        grads[2, :, hc] = jnp.dot(p.astype(BF16), do, preferred_element_type=F32).astype(BF16)
        for a in range(3):
            for t in (2, 3, 1):
                home(a, t, hc, s * width + h * HEAD_DIM, HEAD_DIM).start()
        return carry

    def differentiate(c):
        cc = pl.ds(c * TILE, TILE)
        got_p[0, c].wait_recv()
        got_z[c].wait_recv()
        dout[:, cc] = (keep[0, :, cc] + pgot[0, :, cc].astype(F32) + zgot[:, cc].astype(F32)).astype(BF16)
        lax.fori_loop(c * per, (c + 1) * per, backward, 0)

    for c in range(chunks - 1):
        differentiate(c)

    def weight_tile(start):
        total = jnp.zeros((width, TILE), F32)
        for r in range(4):
            total += jnp.dot(att[r], g[r, :, pl.ds(start, TILE)], preferred_element_type=F32)
        return total

    for c in range(chunks):
        got_att[1, c].wait_recv()
        got_att[3, c].wait_recv()
    got_gw = []
    for c in range(block // TILE):
        cc = pl.ds(c * TILE, TILE)
        gwsend[:, cc] = weight_tile(block + c * TILE).astype(BF16)
        got_gw.append(push(gwsend.at[:, cc], gwgot.at[:, cc], far))
    differentiate(chunks - 1)
    for c in range(block // TILE):
        gw_out[:, pl.ds(c * TILE, TILE)] = weight_tile(c * TILE)

    last = [here(grads.at[a, rows(0)], outs[a].at[0, :, cols(s, width)]) for a in range(3)]
    for copy in got_gw:
        copy.wait_recv()
    gw_out[...] += gwgot[...].astype(F32)
    for a in range(3):
        for t in (1, 2, 3):
            whole = home(a, t, pl.ds(0, width), s * width, width)
            whole.wait_send()
            whole.wait_recv()
    for copy in last:
        copy.wait()
    for copy in pending:
        copy.wait_send()


def fused(queries, attn_keys, attn_values, grad_out, out_weight):
    tokens = queries.shape[1]
    length = tokens * lax.axis_size("seq")
    width, block = out_weight.shape
    heads = width // HEAD_DIM
    any_spec = pl.BlockSpec(memory_space=pl.ANY)
    flops = 4 * length * width * grad_out.shape[2] + 12 * heads * length * length * HEAD_DIM
    results = pl.pallas_call(
        kernel,
        out_shape=(
            jax.ShapeDtypeStruct(queries.shape, BF16),
            jax.ShapeDtypeStruct(queries.shape, BF16),
            jax.ShapeDtypeStruct(queries.shape, BF16),
            jax.ShapeDtypeStruct(out_weight.shape, F32),
        ),
        in_specs=[any_spec] * 5,
        out_specs=(any_spec, any_spec, any_spec, pl.BlockSpec(memory_space=pltpu.VMEM)),
        scratch_shapes=[
            pltpu.VMEM((3, length, width), BF16),
            pltpu.VMEM((4, length, 2 * block), BF16),
            pltpu.VMEM((width, 2 * block), BF16),
            pltpu.VMEM((4, width, length), BF16),
            pltpu.VMEM((heads, length, length), F32),
            pltpu.VMEM((2, length, width), F32),
            pltpu.VMEM((2, length, width), BF16),
            pltpu.VMEM((2, length, width), BF16),
            pltpu.VMEM((length, width), BF16),
            pltpu.VMEM((length, width), BF16),
            pltpu.VMEM((length, width), BF16),
            pltpu.VMEM((3, length, width), BF16),
            pltpu.VMEM((width, block), BF16),
            pltpu.VMEM((width, block), BF16),
            pltpu.SemaphoreType.DMA((96,)),
            pltpu.SemaphoreType.DMA((96,)),
            pltpu.SemaphoreType.DMA((16,)),
        ],
        compiler_params=pltpu.CompilerParams(
            collective_id=0, has_side_effects=True, vmem_limit_bytes=60 * 1024 * 1024
        ),
        cost_estimate=pl.CostEstimate(flops=flops, bytes_accessed=20 * 1024 * 1024, transcendentals=0),
    )(queries, attn_keys, attn_values, grad_out, out_weight)
    return place(*results)


def place_kernel(*refs):
    for src, dst in zip(refs[:4], refs[4:]):
        dst[...] = src[...]


def place(*results):
    steps = 4
    specs = [pl.BlockSpec((1, x.shape[1] // steps, x.shape[2]), lambda i: (0, i, 0)) for x in results[:3]]
    specs.append(pl.BlockSpec((results[3].shape[0] // steps, results[3].shape[1]), lambda i: (i, 0)))
    return pl.pallas_call(
        place_kernel,
        grid=(steps,),
        out_shape=tuple(jax.ShapeDtypeStruct(x.shape, x.dtype) for x in results),
        in_specs=specs,
        out_specs=tuple(specs),
        compiler_params=pltpu.CompilerParams(vmem_limit_bytes=60 * 1024 * 1024),
    )(*results)


def head_pass(q, k, v, dout):
    scale = 1.0 / q.shape[1] ** 0.5
    scores = jnp.dot(q, k.T, preferred_element_type=F32) * scale
    expo = jnp.exp(scores - jnp.max(scores, axis=1, keepdims=True))
    probs = expo / jnp.sum(expo, axis=1, keepdims=True)
    probs_low = probs.astype(BF16)
    attended = jnp.dot(probs_low, v, preferred_element_type=F32).astype(BF16)
    grad_v = jnp.dot(probs_low.T, dout, preferred_element_type=F32).astype(BF16)
    grad_probs = jnp.dot(dout, v.T, preferred_element_type=F32)
    delta = jnp.sum(dout.astype(F32) * attended.astype(F32), axis=1, keepdims=True)
    grad_scores = (probs * (grad_probs - delta)).astype(BF16)
    grad_q = (jnp.dot(grad_scores, k, preferred_element_type=F32) * scale).astype(BF16)
    grad_k = (jnp.dot(grad_scores.T, q, preferred_element_type=F32) * scale).astype(BF16)
    return attended, grad_q, grad_k, grad_v


def collectives(queries, attn_keys, attn_values, grad_out, out_weight):
    width = queries.shape[2] // lax.axis_size("seq")
    q, k, v = (
        lax.all_to_all(x, "seq", split_axis=2, concat_axis=1, tiled=True)[0]
        for x in (queries, attn_keys, attn_values)
    )
    every_rows = lax.all_gather(grad_out, "seq", axis=1, tiled=True)
    flat_rows = every_rows.reshape(-1, every_rows.shape[2])
    weight = lax.all_gather(out_weight, "fsdp", axis=1, tiled=True)
    dout = lax.dot_general(flat_rows, weight, NT, preferred_element_type=F32).astype(BF16)
    pieces = []
    for lower in range(0, width, HEAD_DIM):
        here = slice(lower, lower + HEAD_DIM)
        pieces.append(head_pass(q[:, here], k[:, here], v[:, here], dout[:, here]))
    attended = jnp.concatenate([item[0] for item in pieces], axis=1)
    grads = [
        lax.all_to_all(
            jnp.concatenate([item[i] for item in pieces], axis=1)[None],
            "seq", split_axis=1, concat_axis=2, tiled=True,
        )
        for i in (1, 2, 3)
    ]
    whole = lax.dot_general(attended, flat_rows, TN, preferred_element_type=F32)
    return (*grads, lax.psum_scatter(whole, "fsdp", scatter_dimension=1, tiled=True))


def shards(queries, attn_keys, attn_values, grad_out, out_weight):
    width, block = out_weight.shape
    fits = lax.axis_size("seq") == 4 and lax.axis_size("fsdp") == 8
    if fits and queries.shape[0] == 1 and queries.shape[1] % 64 == 0 and width % TILE == 0 and block % TILE == 0:
        return fused(queries, attn_keys, attn_values, grad_out, out_weight)
    return collectives(queries, attn_keys, attn_values, grad_out, out_weight)


def solution(mesh):
    return jax.shard_map(
        shards,
        mesh=mesh,
        in_specs=(
            P("fsdp", "seq", None),
            P("fsdp", "seq", None),
            P("fsdp", "seq", None),
            P("fsdp", "seq", None),
            P("seq", "fsdp"),
        ),
        out_specs=(
            P("fsdp", "seq", None),
            P("fsdp", "seq", None),
            P("fsdp", "seq", None),
            P("seq", "fsdp"),
        ),
        check_vma=False,
    )
```

```python
import jax
import jax.numpy as jnp
from jax import lax
from jax.experimental import pallas as pl
from jax.experimental.pallas import tpu as pltpu
from jax.sharding import PartitionSpec as P

HEAD_DIM = 128
LOG2_E = 1.4426950408889634
TILE = 256
MESH = pl.DeviceIdType.MESH
F32, BF16 = jnp.float32, jnp.bfloat16
NT = (((1,), (1,)), ((), ()))
TN = (((0,), (0,)), ((), ()))


def kernel(
    q_ref, k_ref, v_ref, go_ref, w_ref,
    gq_out, gk_out, gv_out, gw_out,
    qkv, g, w, att, probs, keep, psend, pgot, zsend, zgot, dout, grads, gwsend, gwgot,
    send, recv, local,
):
    s, f = lax.axis_index("seq"), lax.axis_index("fsdp")
    tokens = q_ref.shape[1]
    width = w_ref.shape[0]
    block = w_ref.shape[1]
    heads = width // HEAD_DIM
    scale = 1.0 / HEAD_DIM**0.5
    core = s + 1 - 2 * (s % 2)
    across = s + 2 - 4 * (s // 2)
    both = core + 2 - 4 * (core // 2)
    f_y = f + 1 - 2 * (f % 2)
    f_z = f + 4 - 8 * (f // 4)
    f_yz = f_z + 1 - 2 * (f_z % 2)

    def other_half(i):
        return i + 2 - 4 * ((i // 2) % 2)

    tok_peer = [None] + [{"seq": i, "fsdp": f} for i in (core, across, both)]
    tok_id = [s, core, across, both]
    row_peer = [None] + [{"seq": s, "fsdp": i} for i in (f_y, f_z, f_yz)]
    row_id = [f, f_y, f_z, f_yz]
    far = {"seq": s, "fsdp": other_half(f)}

    barrier = pltpu.get_barrier_semaphore()
    peers = tok_peer[1:] + row_peer[1:] + [far]
    for peer in peers:
        pl.semaphore_signal(barrier, inc=1, device_id=peer, device_id_type=MESH)
    pl.semaphore_wait(barrier, len(peers))

    count = [0, 0]
    pending = []

    def push(src, dst, peer):
        i = count[0]
        count[0] += 1
        copy = pltpu.make_async_remote_copy(
            src_ref=src, dst_ref=dst, send_sem=send.at[i], recv_sem=recv.at[i],
            device_id=peer, device_id_type=MESH,
        )
        copy.start()
        pending.append(copy)
        return copy

    def here(src, dst):
        i = count[1]
        count[1] += 1
        copy = pltpu.make_async_copy(src, dst, local.at[i])
        copy.start()
        return copy

    def cols(i, size):
        return pl.ds(pl.multiple_of(i * size, 128), size)

    def rows(t):
        return pl.ds(t * tokens, tokens)

    own = []
    for c in range(2):
        owner = f if c == 0 else other_half(f)
        own.append(here(go_ref.at[0, :, cols(owner, block)], g.at[0, rows(0), pl.ds(c * block, block)]))
    got_g = {}
    for r in (1, 3, 2):
        for c in range(2):
            owner = row_id[r] if c == 0 else other_half(row_id[r])
            got_g[r, c] = push(
                go_ref.at[0, :, cols(owner, block)], g.at[r, rows(0), pl.ds(c * block, block)], row_peer[r]
            )
    chunks = width // TILE
    per = TILE // HEAD_DIM
    got_qkv, own_qkv = {}, []

    def send_qkv(c):
        cc = pl.ds(c * TILE, TILE)
        got_qkv[c] = []
        for a, ref in enumerate((q_ref, k_ref, v_ref)):
            for t in (2, 3, 1):
                start = pl.multiple_of(tok_id[t] * width + c * TILE, 128)
                got_qkv[c].append(
                    push(ref.at[0, :, pl.ds(start, TILE)], qkv.at[a, rows(t), cc], tok_peer[t])
                )

    send_qkv(0)
    for a, ref in enumerate((q_ref, k_ref, v_ref)):
        own_qkv.append(here(ref.at[0, :, cols(s, width)], qkv.at[a, rows(0)]))
    got_w = push(w_ref, w.at[:, pl.ds(block, block)], far)
    own_w = here(w_ref, w.at[:, pl.ds(0, block)])

    got_g2 = {}

    def spread(r):
        for t in (2, 1):
            got_g2[r, t] = push(g.at[r, rows(0)], g.at[r, rows(t)], tok_peer[t])

    for copy in own + own_qkv:
        copy.wait()

    def arrived(r):
        got_g[r, 0].wait_recv()
        got_g[r, 1].wait_recv()
        spread(r)

    spread(0)
    arrived(1)
    for c in range(1, chunks):
        send_qkv(c)

    def forward(h, carry):
        hc = cols(h, HEAD_DIM)
        scores = lax.dot_general(qkv[1, :, hc], qkv[0, :, hc], NT, preferred_element_type=F32)
        top = jnp.max(scores, axis=0, keepdims=True) * (scale * LOG2_E)
        expo = jnp.exp2(scores * (scale * LOG2_E) - top)
        p = expo * (1.0 / jnp.sum(expo, axis=0, keepdims=True))
        probs[h] = p
        att[0, hc, :] = lax.dot_general(
            qkv[2, :, hc], p.astype(BF16), TN, preferred_element_type=F32
        ).astype(BF16)
        return carry

    got_att = {}

    def attend(c):
        for copy in got_qkv[c]:
            copy.wait_recv()
        lax.fori_loop(c * per, (c + 1) * per, forward, 0)
        cc = pl.ds(c * TILE, TILE)
        got_att[1, c] = push(att.at[0, cc], att.at[1, cc], row_peer[1])
        got_att[2, c] = push(att.at[0, cc], att.at[2, cc], row_peer[2])

    for c in range(chunks - 1):
        attend(c)
    arrived(3)
    arrived(2)
    attend(chunks - 1)

    def across_done(r):
        got_g2[r, 2].wait_recv()
        got_g2[r, 3] = push(g.at[r, rows(2)], g.at[r, rows(3)], tok_peer[1])

    def relay(c):
        got_att[2, c].wait_recv()
        cc = pl.ds(c * TILE, TILE)
        got_att[3, c] = push(att.at[2, cc], att.at[3, cc], row_peer[1])

    for c in range(chunks - 1):
        relay(c)
    across_done(0)
    across_done(1)
    own_w.wait()
    got_w.wait_recv()

    def partial(r, c):
        return lax.dot_general(g[r], w[pl.ds(c * TILE, TILE), :], NT, preferred_element_type=F32)

    def whole_rows(r):
        got_g2[r, 1].wait_recv()
        got_g2[r, 3].wait_recv()

    got_p = {}

    def send_partial(slot, r):
        whole_rows(r)
        for c in range(chunks):
            cc = pl.ds(c * TILE, TILE)
            psend[slot, :, cc] = partial(r, c).astype(BF16)
            got_p[slot, c] = push(psend.at[slot, :, cc], pgot.at[slot, :, cc], row_peer[1])

    def keep_partial(slot, r):
        whole_rows(r)
        for c in range(chunks):
            keep[slot, :, pl.ds(c * TILE, TILE)] = partial(r, c)

    send_partial(0, 1)
    relay(chunks - 1)
    keep_partial(0, 0)
    across_done(3)
    across_done(2)
    send_partial(1, 3)
    keep_partial(1, 2)

    def weight_tile(start):
        total = jnp.zeros((width, TILE), F32)
        for r in range(4):
            total += jnp.dot(att[r], g[r, :, pl.ds(start, TILE)], preferred_element_type=F32)
        return total

    for c in range(chunks):
        got_att[1, c].wait_recv()
        got_att[3, c].wait_recv()
    got_gw = []
    for c in range(block // TILE):
        cc = pl.ds(c * TILE, TILE)
        gwsend[:, cc] = weight_tile(block + c * TILE).astype(BF16)
        got_gw.append(push(gwsend.at[:, cc], gwgot.at[:, cc], far))

    got_z = []
    for c in range(chunks):
        cc = pl.ds(c * TILE, TILE)
        got_p[1, c].wait_recv()
        zsend[:, cc] = (keep[1, :, cc] + pgot[1, :, cc].astype(F32)).astype(BF16)
        got_z.append(push(zsend.at[:, cc], zgot.at[:, cc], row_peer[2]))

    for c in range(block // TILE):
        gw_out[:, pl.ds(c * TILE, TILE)] = weight_tile(c * TILE)

    outs = (gq_out, gk_out, gv_out)
    base = count[0]
    count[0] += 9

    def home(a, t, hc, start, size):
        i = base + a * 3 + t - 1
        return pltpu.make_async_remote_copy(
            src_ref=grads.at[a, rows(t), hc],
            dst_ref=outs[a].at[0, :, pl.ds(pl.multiple_of(start, 128), size)],
            send_sem=send.at[i], recv_sem=recv.at[i],
            device_id=tok_peer[t], device_id_type=MESH,
        )

    def backward(h, carry):
        hc = cols(h, HEAD_DIM)
        q, k, v, do = qkv[0, :, hc], qkv[1, :, hc], qkv[2, :, hc], dout[:, hc]
        p = probs[h]
        delta = jnp.sum(do.astype(F32).T * att[0, hc, :].astype(F32), axis=0, keepdims=True)
        grad_p = lax.dot_general(v, do, NT, preferred_element_type=F32)
        grad_s = (p * (grad_p - delta)).astype(BF16)
        grad_q = lax.dot_general(k, grad_s, TN, preferred_element_type=F32) * scale
        grads[0, :, hc] = grad_q.T.astype(BF16)
        grads[1, :, hc] = (jnp.dot(grad_s, q, preferred_element_type=F32) * scale).astype(BF16)
        grads[2, :, hc] = jnp.dot(p.astype(BF16), do, preferred_element_type=F32).astype(BF16)
        for a in range(3):
            for t in (2, 3, 1):
                home(a, t, hc, s * width + h * HEAD_DIM, HEAD_DIM).start()
        return carry

    def differentiate(c):
        cc = pl.ds(c * TILE, TILE)
        got_p[0, c].wait_recv()
        got_z[c].wait_recv()
        dout[:, cc] = (keep[0, :, cc] + pgot[0, :, cc].astype(F32) + zgot[:, cc].astype(F32)).astype(BF16)
        lax.fori_loop(c * per, (c + 1) * per, backward, 0)

    for c in range(chunks):
        differentiate(c)

    last = [here(grads.at[a, rows(0)], outs[a].at[0, :, cols(s, width)]) for a in range(3)]
    for copy in got_gw:
        copy.wait_recv()
    gw_out[...] += gwgot[...].astype(F32)
    for a in range(3):
        for t in (1, 2, 3):
            whole = home(a, t, pl.ds(0, width), s * width, width)
            whole.wait_send()
            whole.wait_recv()
    for copy in last:
        copy.wait()
    for copy in pending:
        copy.wait_send()


def fused(queries, attn_keys, attn_values, grad_out, out_weight):
    tokens = queries.shape[1]
    length = tokens * lax.axis_size("seq")
    width, block = out_weight.shape
    heads = width // HEAD_DIM
    any_spec = pl.BlockSpec(memory_space=pl.ANY)
    flops = 4 * length * width * grad_out.shape[2] + 12 * heads * length * length * HEAD_DIM
    results = pl.pallas_call(
        kernel,
        out_shape=(
            jax.ShapeDtypeStruct(queries.shape, BF16),
            jax.ShapeDtypeStruct(queries.shape, BF16),
            jax.ShapeDtypeStruct(queries.shape, BF16),
            jax.ShapeDtypeStruct(out_weight.shape, F32),
        ),
        in_specs=[any_spec] * 5,
        out_specs=(any_spec, any_spec, any_spec, pl.BlockSpec(memory_space=pltpu.VMEM)),
        scratch_shapes=[
            pltpu.VMEM((3, length, width), BF16),
            pltpu.VMEM((4, length, 2 * block), BF16),
            pltpu.VMEM((width, 2 * block), BF16),
            pltpu.VMEM((4, width, length), BF16),
            pltpu.VMEM((heads, length, length), F32),
            pltpu.VMEM((2, length, width), F32),
            pltpu.VMEM((2, length, width), BF16),
            pltpu.VMEM((2, length, width), BF16),
            pltpu.VMEM((length, width), BF16),
            pltpu.VMEM((length, width), BF16),
            pltpu.VMEM((length, width), BF16),
            pltpu.VMEM((3, length, width), BF16),
            pltpu.VMEM((width, block), BF16),
            pltpu.VMEM((width, block), BF16),
            pltpu.SemaphoreType.DMA((96,)),
            pltpu.SemaphoreType.DMA((96,)),
            pltpu.SemaphoreType.DMA((16,)),
        ],
        compiler_params=pltpu.CompilerParams(
            collective_id=0, has_side_effects=True, vmem_limit_bytes=60 * 1024 * 1024
        ),
        cost_estimate=pl.CostEstimate(flops=flops, bytes_accessed=20 * 1024 * 1024, transcendentals=0),
    )(queries, attn_keys, attn_values, grad_out, out_weight)
    return place(*results)


def place_kernel(*refs):
    for src, dst in zip(refs[:4], refs[4:]):
        dst[...] = src[...]


def place(*results):
    steps = 4
    specs = [pl.BlockSpec((1, x.shape[1] // steps, x.shape[2]), lambda i: (0, i, 0)) for x in results[:3]]
    specs.append(pl.BlockSpec((results[3].shape[0] // steps, results[3].shape[1]), lambda i: (i, 0)))
    return pl.pallas_call(
        place_kernel,
        grid=(steps,),
        out_shape=tuple(jax.ShapeDtypeStruct(x.shape, x.dtype) for x in results),
        in_specs=specs,
        out_specs=tuple(specs),
        compiler_params=pltpu.CompilerParams(vmem_limit_bytes=60 * 1024 * 1024),
    )(*results)


def head_pass(q, k, v, dout):
    scale = 1.0 / q.shape[1] ** 0.5
    scores = jnp.dot(q, k.T, preferred_element_type=F32) * scale
    expo = jnp.exp(scores - jnp.max(scores, axis=1, keepdims=True))
    probs = expo / jnp.sum(expo, axis=1, keepdims=True)
    probs_low = probs.astype(BF16)
    attended = jnp.dot(probs_low, v, preferred_element_type=F32).astype(BF16)
    grad_v = jnp.dot(probs_low.T, dout, preferred_element_type=F32).astype(BF16)
    grad_probs = jnp.dot(dout, v.T, preferred_element_type=F32)
    delta = jnp.sum(dout.astype(F32) * attended.astype(F32), axis=1, keepdims=True)
    grad_scores = (probs * (grad_probs - delta)).astype(BF16)
    grad_q = (jnp.dot(grad_scores, k, preferred_element_type=F32) * scale).astype(BF16)
    grad_k = (jnp.dot(grad_scores.T, q, preferred_element_type=F32) * scale).astype(BF16)
    return attended, grad_q, grad_k, grad_v


def collectives(queries, attn_keys, attn_values, grad_out, out_weight):
    width = queries.shape[2] // lax.axis_size("seq")
    q, k, v = (
        lax.all_to_all(x, "seq", split_axis=2, concat_axis=1, tiled=True)[0]
        for x in (queries, attn_keys, attn_values)
    )
    every_rows = lax.all_gather(grad_out, "seq", axis=1, tiled=True)
    flat_rows = every_rows.reshape(-1, every_rows.shape[2])
    weight = lax.all_gather(out_weight, "fsdp", axis=1, tiled=True)
    dout = lax.dot_general(flat_rows, weight, NT, preferred_element_type=F32).astype(BF16)
    pieces = []
    for lower in range(0, width, HEAD_DIM):
        here = slice(lower, lower + HEAD_DIM)
        pieces.append(head_pass(q[:, here], k[:, here], v[:, here], dout[:, here]))
    attended = jnp.concatenate([item[0] for item in pieces], axis=1)
    grads = [
        lax.all_to_all(
            jnp.concatenate([item[i] for item in pieces], axis=1)[None],
            "seq", split_axis=1, concat_axis=2, tiled=True,
        )
        for i in (1, 2, 3)
    ]
    whole = lax.dot_general(attended, flat_rows, TN, preferred_element_type=F32)
    return (*grads, lax.psum_scatter(whole, "fsdp", scatter_dimension=1, tiled=True))


def shards(queries, attn_keys, attn_values, grad_out, out_weight):
    width, block = out_weight.shape
    fits = lax.axis_size("seq") == 4 and lax.axis_size("fsdp") == 8
    if fits and queries.shape[0] == 1 and queries.shape[1] % 64 == 0 and width % TILE == 0 and block % TILE == 0:
        return fused(queries, attn_keys, attn_values, grad_out, out_weight)
    return collectives(queries, attn_keys, attn_values, grad_out, out_weight)


def solution(mesh):
    return jax.shard_map(
        shards,
        mesh=mesh,
        in_specs=(
            P("fsdp", "seq", None),
            P("fsdp", "seq", None),
            P("fsdp", "seq", None),
            P("fsdp", "seq", None),
            P("seq", "fsdp"),
        ),
        out_specs=(
            P("fsdp", "seq", None),
            P("fsdp", "seq", None),
            P("fsdp", "seq", None),
            P("seq", "fsdp"),
        ),
        check_vma=False,
    )
```

```python
import jax
import jax.numpy as jnp
from jax import lax
from jax.experimental import pallas as pl
from jax.experimental.pallas import tpu as pltpu
from jax.sharding import PartitionSpec as P

HEAD_DIM = 128
LOG2_E = 1.4426950408889634
TILE = 256
MESH = pl.DeviceIdType.MESH
F32, BF16 = jnp.float32, jnp.bfloat16
NT = (((1,), (1,)), ((), ()))
TN = (((0,), (0,)), ((), ()))


def kernel(
    q_ref, k_ref, v_ref, go_ref, w_ref,
    gq_out, gk_out, gv_out, gw_out,
    qkv, g, w, att, probs, keep, psend, pgot, zsend, zgot, dout, grads, gwsend, gwgot,
    send, recv, local,
):
    s, f = lax.axis_index("seq"), lax.axis_index("fsdp")
    tokens = q_ref.shape[1]
    width = w_ref.shape[0]
    block = w_ref.shape[1]
    heads = width // HEAD_DIM
    scale = 1.0 / HEAD_DIM**0.5
    core = s + 1 - 2 * (s % 2)
    across = s + 2 - 4 * (s // 2)
    both = core + 2 - 4 * (core // 2)
    f_y = f + 1 - 2 * (f % 2)
    f_z = f + 2 - 4 * ((f // 2) % 2)
    f_yz = f_z + 1 - 2 * (f_z % 2)

    def other_half(i):
        return i + 4 - 8 * (i // 4)

    tok_peer = [None] + [{"seq": i, "fsdp": f} for i in (core, across, both)]
    tok_id = [s, core, across, both]
    row_peer = [None] + [{"seq": s, "fsdp": i} for i in (f_y, f_z, f_yz)]
    row_id = [f, f_y, f_z, f_yz]
    far = {"seq": s, "fsdp": other_half(f)}

    barrier = pltpu.get_barrier_semaphore()
    peers = tok_peer[1:] + row_peer[1:] + [far]
    for peer in peers:
        pl.semaphore_signal(barrier, inc=1, device_id=peer, device_id_type=MESH)
    pl.semaphore_wait(barrier, len(peers))

    count = [0, 0]
    pending = []

    def push(src, dst, peer):
        i = count[0]
        count[0] += 1
        copy = pltpu.make_async_remote_copy(
            src_ref=src, dst_ref=dst, send_sem=send.at[i], recv_sem=recv.at[i],
            device_id=peer, device_id_type=MESH,
        )
        copy.start()
        pending.append(copy)
        return copy

    def here(src, dst):
        i = count[1]
        count[1] += 1
        copy = pltpu.make_async_copy(src, dst, local.at[i])
        copy.start()
        return copy

    def cols(i, size):
        return pl.ds(pl.multiple_of(i * size, 128), size)

    def rows(t):
        return pl.ds(t * tokens, tokens)

    own = []
    for c in range(2):
        owner = f if c == 0 else other_half(f)
        own.append(here(go_ref.at[0, :, cols(owner, block)], g.at[0, rows(0), pl.ds(c * block, block)]))
    got_g = {}
    for r in (3, 1, 2):
        for c in range(2):
            owner = row_id[r] if c == 0 else other_half(row_id[r])
            got_g[r, c] = push(
                go_ref.at[0, :, cols(owner, block)], g.at[r, rows(0), pl.ds(c * block, block)], row_peer[r]
            )
    chunks = width // TILE
    per = TILE // HEAD_DIM
    got_qkv, own_qkv = {}, []
    for c in range(chunks):
        cc = pl.ds(c * TILE, TILE)
        got_qkv[c] = []
        for a, ref in enumerate((q_ref, k_ref, v_ref)):
            for t in (2, 3, 1):
                start = pl.multiple_of(tok_id[t] * width + c * TILE, 128)
                got_qkv[c].append(
                    push(ref.at[0, :, pl.ds(start, TILE)], qkv.at[a, rows(t), cc], tok_peer[t])
                )
    for a, ref in enumerate((q_ref, k_ref, v_ref)):
        own_qkv.append(here(ref.at[0, :, cols(s, width)], qkv.at[a, rows(0)]))
    got_w = push(w_ref, w.at[:, pl.ds(block, block)], far)
    own_w = here(w_ref, w.at[:, pl.ds(0, block)])

    got_g2 = {}

    def spread(r):
        for t in (2, 1):
            got_g2[r, t] = push(g.at[r, rows(0)], g.at[r, rows(t)], tok_peer[t])

    for copy in own + own_qkv:
        copy.wait()

    def forward(h, carry):
        hc = cols(h, HEAD_DIM)
        scores = lax.dot_general(qkv[1, :, hc], qkv[0, :, hc], NT, preferred_element_type=F32)
        top = jnp.max(scores, axis=0, keepdims=True) * (scale * LOG2_E)
        expo = jnp.exp2(scores * (scale * LOG2_E) - top)
        p = expo * (1.0 / jnp.sum(expo, axis=0, keepdims=True))
        probs[h] = p
        att[0, hc, :] = lax.dot_general(
            qkv[2, :, hc], p.astype(BF16), TN, preferred_element_type=F32
        ).astype(BF16)
        return carry

    order = (0, 3, 1, 2)
    groups = [order[4 * c // chunks : 4 * (c + 1) // chunks] for c in range(chunks)]
    got_att = {}
    for c in range(chunks):
        for copy in got_qkv[c]:
            copy.wait_recv()
        for r in groups[c]:
            if r:
                got_g[r, 0].wait_recv()
                got_g[r, 1].wait_recv()
            spread(r)
        lax.fori_loop(c * per, (c + 1) * per, forward, 0)
        cc = pl.ds(c * TILE, TILE)
        got_att[1, c] = push(att.at[0, cc], att.at[1, cc], row_peer[1])
        got_att[2, c] = push(att.at[0, cc], att.at[2, cc], row_peer[2])

    def across_done(r):
        got_g2[r, 2].wait_recv()
        got_g2[r, 3] = push(g.at[r, rows(2)], g.at[r, rows(3)], tok_peer[1])

    def relay(c):
        got_att[2, c].wait_recv()
        cc = pl.ds(c * TILE, TILE)
        got_att[3, c] = push(att.at[2, cc], att.at[3, cc], row_peer[1])

    for c in range(chunks - 1):
        relay(c)
    for r in order[:3]:
        across_done(r)
    own_w.wait()
    got_w.wait_recv()

    def partial(r, c):
        return lax.dot_general(g[r], w[pl.ds(c * TILE, TILE), :], NT, preferred_element_type=F32)

    def whole_rows(r):
        got_g2[r, 1].wait_recv()
        got_g2[r, 3].wait_recv()

    got_p = {}
    for slot, r in ((1, 3), (0, 1)):
        whole_rows(r)
        for c in range(chunks):
            cc = pl.ds(c * TILE, TILE)
            psend[slot, :, cc] = partial(r, c).astype(BF16)
            got_p[slot, c] = push(psend.at[slot, :, cc], pgot.at[slot, :, cc], row_peer[1])
        if r == 3:
            relay(chunks - 1)
            across_done(2)
    whole_rows(2)
    whole_rows(0)
    for c in range(chunks):
        got_att[1, c].wait_recv()
        got_att[3, c].wait_recv()

    def weight_tile(start):
        total = jnp.zeros((width, TILE), F32)
        for r in range(4):
            total += jnp.dot(att[r], g[r, :, pl.ds(start, TILE)], preferred_element_type=F32)
        return total

    got_gw = []
    for c in range(block // TILE):
        cc = pl.ds(c * TILE, TILE)
        gwsend[:, cc] = weight_tile(block + c * TILE).astype(BF16)
        got_gw.append(push(gwsend.at[:, cc], gwgot.at[:, cc], far))

    for slot, r in ((1, 2), (0, 0)):
        for c in range(chunks):
            keep[slot, :, pl.ds(c * TILE, TILE)] = partial(r, c)

    got_z = []
    for c in range(chunks):
        cc = pl.ds(c * TILE, TILE)
        got_p[1, c].wait_recv()
        zsend[:, cc] = (keep[1, :, cc] + pgot[1, :, cc].astype(F32)).astype(BF16)
        got_z.append(push(zsend.at[:, cc], zgot.at[:, cc], row_peer[2]))

    for c in range(block // TILE):
        gw_out[:, pl.ds(c * TILE, TILE)] = weight_tile(c * TILE)

    outs = (gq_out, gk_out, gv_out)
    base = count[0]
    count[0] += 9

    def home(a, t, hc, start, size):
        i = base + a * 3 + t - 1
        return pltpu.make_async_remote_copy(
            src_ref=grads.at[a, rows(t), hc],
            dst_ref=outs[a].at[0, :, pl.ds(pl.multiple_of(start, 128), size)],
            send_sem=send.at[i], recv_sem=recv.at[i],
            device_id=tok_peer[t], device_id_type=MESH,
        )

    def backward(h, carry):
        hc = cols(h, HEAD_DIM)
        q, k, v, do = qkv[0, :, hc], qkv[1, :, hc], qkv[2, :, hc], dout[:, hc]
        p = probs[h]
        delta = jnp.sum(do.astype(F32).T * att[0, hc, :].astype(F32), axis=0, keepdims=True)
        grad_p = lax.dot_general(v, do, NT, preferred_element_type=F32)
        grad_s = (p * (grad_p - delta)).astype(BF16)
        grad_q = lax.dot_general(k, grad_s, TN, preferred_element_type=F32) * scale
        grads[0, :, hc] = grad_q.T.astype(BF16)
        grads[1, :, hc] = (jnp.dot(grad_s, q, preferred_element_type=F32) * scale).astype(BF16)
        grads[2, :, hc] = jnp.dot(p.astype(BF16), do, preferred_element_type=F32).astype(BF16)
        for a in range(3):
            for t in (2, 3, 1):
                home(a, t, hc, s * width + h * HEAD_DIM, HEAD_DIM).start()
        return carry

    for c in range(chunks):
        cc = pl.ds(c * TILE, TILE)
        got_p[0, c].wait_recv()
        got_z[c].wait_recv()
        dout[:, cc] = (keep[0, :, cc] + pgot[0, :, cc].astype(F32) + zgot[:, cc].astype(F32)).astype(BF16)
        lax.fori_loop(c * per, (c + 1) * per, backward, 0)

    last = [here(grads.at[a, rows(0)], outs[a].at[0, :, cols(s, width)]) for a in range(3)]
    for copy in got_gw:
        copy.wait_recv()
    gw_out[...] += gwgot[...].astype(F32)
    for a in range(3):
        for t in (1, 2, 3):
            whole = home(a, t, pl.ds(0, width), s * width, width)
            whole.wait_send()
            whole.wait_recv()
    for copy in last:
        copy.wait()
    for copy in pending:
        copy.wait_send()


def fused(queries, attn_keys, attn_values, grad_out, out_weight):
    tokens = queries.shape[1]
    length = tokens * lax.axis_size("seq")
    width, block = out_weight.shape
    heads = width // HEAD_DIM
    any_spec = pl.BlockSpec(memory_space=pl.ANY)
    flops = 4 * length * width * grad_out.shape[2] + 12 * heads * length * length * HEAD_DIM
    results = pl.pallas_call(
        kernel,
        out_shape=(
            jax.ShapeDtypeStruct(queries.shape, BF16),
            jax.ShapeDtypeStruct(queries.shape, BF16),
            jax.ShapeDtypeStruct(queries.shape, BF16),
            jax.ShapeDtypeStruct(out_weight.shape, F32),
        ),
        in_specs=[any_spec] * 5,
        out_specs=(any_spec, any_spec, any_spec, pl.BlockSpec(memory_space=pltpu.VMEM)),
        scratch_shapes=[
            pltpu.VMEM((3, length, width), BF16),
            pltpu.VMEM((4, length, 2 * block), BF16),
            pltpu.VMEM((width, 2 * block), BF16),
            pltpu.VMEM((4, width, length), BF16),
            pltpu.VMEM((heads, length, length), F32),
            pltpu.VMEM((2, length, width), F32),
            pltpu.VMEM((2, length, width), BF16),
            pltpu.VMEM((2, length, width), BF16),
            pltpu.VMEM((length, width), BF16),
            pltpu.VMEM((length, width), BF16),
            pltpu.VMEM((length, width), BF16),
            pltpu.VMEM((3, length, width), BF16),
            pltpu.VMEM((width, block), BF16),
            pltpu.VMEM((width, block), BF16),
            pltpu.SemaphoreType.DMA((96,)),
            pltpu.SemaphoreType.DMA((96,)),
            pltpu.SemaphoreType.DMA((16,)),
        ],
        compiler_params=pltpu.CompilerParams(
            collective_id=0, has_side_effects=True, vmem_limit_bytes=60 * 1024 * 1024
        ),
        cost_estimate=pl.CostEstimate(flops=flops, bytes_accessed=20 * 1024 * 1024, transcendentals=0),
    )(queries, attn_keys, attn_values, grad_out, out_weight)
    return place(*results)


def place_kernel(*refs):
    for src, dst in zip(refs[:4], refs[4:]):
        dst[...] = src[...]


def place(*results):
    steps = 4
    specs = [pl.BlockSpec((1, x.shape[1] // steps, x.shape[2]), lambda i: (0, i, 0)) for x in results[:3]]
    specs.append(pl.BlockSpec((results[3].shape[0] // steps, results[3].shape[1]), lambda i: (i, 0)))
    return pl.pallas_call(
        place_kernel,
        grid=(steps,),
        out_shape=tuple(jax.ShapeDtypeStruct(x.shape, x.dtype) for x in results),
        in_specs=specs,
        out_specs=tuple(specs),
        compiler_params=pltpu.CompilerParams(vmem_limit_bytes=60 * 1024 * 1024),
    )(*results)


def head_pass(q, k, v, dout):
    scale = 1.0 / q.shape[1] ** 0.5
    scores = jnp.dot(q, k.T, preferred_element_type=F32) * scale
    expo = jnp.exp(scores - jnp.max(scores, axis=1, keepdims=True))
    probs = expo / jnp.sum(expo, axis=1, keepdims=True)
    probs_low = probs.astype(BF16)
    attended = jnp.dot(probs_low, v, preferred_element_type=F32).astype(BF16)
    grad_v = jnp.dot(probs_low.T, dout, preferred_element_type=F32).astype(BF16)
    grad_probs = jnp.dot(dout, v.T, preferred_element_type=F32)
    delta = jnp.sum(dout.astype(F32) * attended.astype(F32), axis=1, keepdims=True)
    grad_scores = (probs * (grad_probs - delta)).astype(BF16)
    grad_q = (jnp.dot(grad_scores, k, preferred_element_type=F32) * scale).astype(BF16)
    grad_k = (jnp.dot(grad_scores.T, q, preferred_element_type=F32) * scale).astype(BF16)
    return attended, grad_q, grad_k, grad_v


def collectives(queries, attn_keys, attn_values, grad_out, out_weight):
    width = queries.shape[2] // lax.axis_size("seq")
    q, k, v = (
        lax.all_to_all(x, "seq", split_axis=2, concat_axis=1, tiled=True)[0]
        for x in (queries, attn_keys, attn_values)
    )
    every_rows = lax.all_gather(grad_out, "seq", axis=1, tiled=True)
    flat_rows = every_rows.reshape(-1, every_rows.shape[2])
    weight = lax.all_gather(out_weight, "fsdp", axis=1, tiled=True)
    dout = lax.dot_general(flat_rows, weight, NT, preferred_element_type=F32).astype(BF16)
    pieces = []
    for lower in range(0, width, HEAD_DIM):
        here = slice(lower, lower + HEAD_DIM)
        pieces.append(head_pass(q[:, here], k[:, here], v[:, here], dout[:, here]))
    attended = jnp.concatenate([item[0] for item in pieces], axis=1)
    grads = [
        lax.all_to_all(
            jnp.concatenate([item[i] for item in pieces], axis=1)[None],
            "seq", split_axis=1, concat_axis=2, tiled=True,
        )
        for i in (1, 2, 3)
    ]
    whole = lax.dot_general(attended, flat_rows, TN, preferred_element_type=F32)
    return (*grads, lax.psum_scatter(whole, "fsdp", scatter_dimension=1, tiled=True))


def shards(queries, attn_keys, attn_values, grad_out, out_weight):
    width, block = out_weight.shape
    fits = lax.axis_size("seq") == 4 and lax.axis_size("fsdp") == 8
    if fits and queries.shape[0] == 1 and queries.shape[1] % 64 == 0 and width % TILE == 0 and block % TILE == 0:
        return fused(queries, attn_keys, attn_values, grad_out, out_weight)
    return collectives(queries, attn_keys, attn_values, grad_out, out_weight)


def solution(mesh):
    return jax.shard_map(
        shards,
        mesh=mesh,
        in_specs=(
            P("fsdp", "seq", None),
            P("fsdp", "seq", None),
            P("fsdp", "seq", None),
            P("fsdp", "seq", None),
            P("seq", "fsdp"),
        ),
        out_specs=(
            P("fsdp", "seq", None),
            P("fsdp", "seq", None),
            P("fsdp", "seq", None),
            P("seq", "fsdp"),
        ),
        check_vma=False,
    )
```
